512 devices in a mesh: ta: 32 (over x_hi, z, core), gx: 16 (over x_lo, y).
Axes of the slice: x: 4 (x_hi: 2, x_lo: 2; x = x_hi * 2 + x_lo), y: 8, z: 8, core: 2. Of those that a mesh axis runs over, the one named last changes fastest.
Arguments:
- source: float32 [24, 128, 64, 128], P(None, 'ta', 'gx'), may hold values from -6 to 6
- gauge_links: float32 [4, 18, 128, 64, 128], P(None, None, 'ta', 'gx'), may hold values from -1 to 1, as said below
Outputs:
- solution: float32 [24, 128, 64, 128], P(None, 'ta', 'gx')
- residual: float32 [24, 128, 64, 128], P(None, 'ta', 'gx')
The draws below stay inside these ranges and needn't reach their ends.
Inputs may be any that keep to these rules, and one draw needn't show every extreme that they name: `gauge_links`: every link, read as a 3x3 complex matrix, is special unitary.
All inputs are finite; a program needn't handle non-finite values.
Results may differ from the reference program's by a relative error of at most 0.00014.
Values sent between devices are 32-bit elements; how exact they have to be, the bound alone decides.
A program may use at most 64 MiB of HBM per device.

```python
import jax
import jax.numpy as jnp
import numpy as np
from jax import lax

BLOCK = 4
LY = 8
LZ = 16
CYCLES = 1
MR_STEPS = 2
NT = 128
NX = 64


def unit_quaternion(key, site_shape):
    quaternion = jax.random.normal(key, (4,) + site_shape, jnp.float32)
    return quaternion / jnp.sqrt(jnp.sum(quaternion * quaternion, axis=0) + 1e-12)


def embed_pair(quaternion, row_first, row_second):
    nought = jnp.zeros_like(quaternion[0])
    unity = jnp.ones_like(quaternion[0])
    real_rows = [[unity if row_index == col_index else nought for col_index in range(3)] for row_index in range(3)]
    imag_rows = [[nought for col_index in range(3)] for row_index in range(3)]
    real_rows[row_first][row_first] = quaternion[0]
    imag_rows[row_first][row_first] = quaternion[1]
    real_rows[row_first][row_second] = quaternion[2]
    imag_rows[row_first][row_second] = quaternion[3]
    real_rows[row_second][row_first] = -quaternion[2]
    imag_rows[row_second][row_first] = quaternion[3]
    real_rows[row_second][row_second] = quaternion[0]
    imag_rows[row_second][row_second] = -quaternion[1]
    return (real_rows, imag_rows)


def complex_product(left_pair, right_pair):
    left_re, left_im = left_pair
    right_re, right_im = right_pair
    out_re = []
    out_im = []
    for row_index in range(3):
        row_re = []
        row_im = []
        for col_index in range(3):
            acc_re = 0.0
            acc_im = 0.0
            for inner_index in range(3):
                acc_re = acc_re + left_re[row_index][inner_index] * right_re[inner_index][col_index] - left_im[row_index][inner_index] * right_im[inner_index][col_index]
                acc_im = acc_im + left_re[row_index][inner_index] * right_im[inner_index][col_index] + left_im[row_index][inner_index] * right_re[inner_index][col_index]
            row_re.append(acc_re)
            row_im.append(acc_im)
        out_re.append(row_re)
        out_im.append(row_im)
    return (out_re, out_im)


def draw_gauge_links(key, part):
    key = jax.random.fold_in(key, 7)
    site_shape = (4, NT, NX, LY * LZ)
    key_one, key_two, key_three = jax.random.split(key, 3)
    first_pair = embed_pair(unit_quaternion(key_one, site_shape), 0, 1)
    second_pair = embed_pair(unit_quaternion(key_two, site_shape), 1, 2)
    third_pair = embed_pair(unit_quaternion(key_three, site_shape), 0, 1)
    product_re, product_im = complex_product(complex_product(first_pair, second_pair), third_pair)
    stacked = jnp.stack([jnp.stack([jnp.stack([product_re[row_index][col_index], product_im[row_index][col_index]]) for col_index in range(3)]) for row_index in range(3)])
    stacked = jnp.moveaxis(stacked, 3, 0)
    return stacked.reshape((4, 18, NT, NX, LY * LZ)).astype(jnp.float32)


def draw_source(key, part):
    key = jax.random.fold_in(key, 11)
    shape_full = (24, NT, NX, LY * LZ)
    return jax.random.truncated_normal(key, -6.0, 6.0, shape_full, jnp.float32)


def setup_inputs(seed: int = 0) -> dict:
    seeds = jax.random.split(jax.random.key(seed), 3)
    return {
        "source": draw_source(jax.random.fold_in(seeds[2], 71), 0),
        "gauge_links": draw_gauge_links(jax.random.fold_in(seeds[2], 71), 0),
    }


GAMMA_PERM = ((2, 3, 0, 1), (3, 2, 1, 0), (3, 2, 1, 0), (2, 3, 0, 1))
GAMMA_PHASE = (((1.0, 0.0), (1.0, 0.0), (1.0, 0.0), (1.0, 0.0)),
               ((0.0, 1.0), (0.0, 1.0), (0.0, -1.0), (0.0, -1.0)),
               ((-1.0, 0.0), (1.0, 0.0), (1.0, 0.0), (-1.0, 0.0)),
               ((0.0, 1.0), (0.0, -1.0), (0.0, -1.0), (0.0, 1.0)))
MASS_SHIFT = 4.1
HOP_SCALE = 0.5
DENOM_EPSILON = 1e-6


def phase_block(phase_re, phase_im):
    return np.array([[phase_re, -phase_im], [phase_im, phase_re]])


def projection_table():
    table = np.zeros((8, 12, 24))
    for direction in range(4):
        for side, parity in ((0, -1.0), (1, 1.0)):
            slot = 2 * direction + side
            for spin_row in (0, 1):
                partner = GAMMA_PERM[direction][spin_row]
                phase_re, phase_im = GAMMA_PHASE[direction][spin_row]
                matrix = parity * phase_block(phase_re, phase_im)
                for colour_idx in range(3):
                    for part_out in range(2):
                        table[slot, 6 * spin_row + 2 * colour_idx + part_out,
                              6 * spin_row + 2 * colour_idx + part_out] += 1.0
                        for part_in in range(2):
                            table[slot, 6 * spin_row + 2 * colour_idx + part_out,
                                  6 * partner + 2 * colour_idx + part_in] += matrix[part_out, part_in]
    return table


def expand_table():
    table = np.zeros((24, 96))
    for direction in range(4):
        for side, parity in ((0, -1.0), (1, 1.0)):
            base = 12 * (2 * direction + side)
            for spin_row in (0, 1):
                for component in range(6):
                    table[6 * spin_row + component, base + 6 * spin_row + component] += -HOP_SCALE
            for spin_row in (2, 3):
                partner = GAMMA_PERM[direction][spin_row]
                phase_re, phase_im = GAMMA_PHASE[direction][spin_row]
                matrix = parity * phase_block(phase_re, phase_im)
                for colour_idx in range(3):
                    for part_out in range(2):
                        for part_in in range(2):
                            table[6 * spin_row + 2 * colour_idx + part_out,
                                  base + 6 * partner + 2 * colour_idx + part_in] += -HOP_SCALE * matrix[part_out, part_in]
    return table


def link_table():
    table = np.zeros((6, 6, 18))
    for row_index in range(3):
        for col_index in range(3):
            real_entry = 6 * row_index + 2 * col_index
            table[2 * row_index, 2 * col_index, real_entry] = 1.0
            table[2 * row_index, 2 * col_index + 1, real_entry + 1] = -1.0
            table[2 * row_index + 1, 2 * col_index, real_entry + 1] = 1.0
            table[2 * row_index + 1, 2 * col_index + 1, real_entry] = 1.0
    return table


def link_matrices(links):
    table = jnp.asarray(link_table(), links.dtype)
    if links.ndim == 5:
        return jnp.einsum('ije,metxf->mijtxf', table, links, precision=lax.Precision.HIGHEST)
    return jnp.einsum('ije,etxf->ijtxf', table, links, precision=lax.Precision.HIGHEST)


def project_all(vector):
    table = jnp.asarray(projection_table(), vector.dtype)
    halves = jnp.einsum('kab,btxf->katxf', table, vector, precision=lax.Precision.HIGHEST)
    return halves.reshape((8, 2, 6) + vector.shape[1:])


def colour_apply(matrix, half):
    return jnp.sum(matrix[None] * half[:, None], axis=2)


def colour_adjoint(matrix, half):
    return jnp.sum(matrix[None] * half[:, :, None], axis=1)


def combine(vector, forward_list, backward_list):
    terms = []
    for direction in range(4):
        terms.append(forward_list[direction])
        terms.append(backward_list[direction])
    stacked = jnp.stack(terms).reshape((96,) + vector.shape[1:])
    table = jnp.asarray(expand_table(), vector.dtype)
    return MASS_SHIFT * vector + jnp.einsum('kb,btxf->ktxf', table, stacked, precision=lax.Precision.HIGHEST)


def neighbour(values, direction, offset, depth_z):
    if direction == 0:
        return jnp.roll(values, -offset, axis=-3)
    if direction == 1:
        return jnp.roll(values, -offset, axis=-2)
    if direction == 2:
        return jnp.roll(values, -offset * depth_z, axis=-1)
    zcoord = lax.broadcasted_iota(jnp.int32, (values.shape[-1],), 0) % depth_z
    if offset == 1:
        return jnp.where(zcoord == depth_z - 1, jnp.roll(values, depth_z - 1, axis=-1), jnp.roll(values, -1, axis=-1))
    return jnp.where(zcoord == 0, jnp.roll(values, 1 - depth_z, axis=-1), jnp.roll(values, 1, axis=-1))


def site_coords(site_shape, depth_z):
    t_size, x_size, flat_size = site_shape
    tcoord = lax.broadcasted_iota(jnp.int32, (t_size, 1, 1), 0)
    xcoord = lax.broadcasted_iota(jnp.int32, (1, x_size, 1), 1)
    flat_coord = lax.broadcasted_iota(jnp.int32, (1, 1, flat_size), 2)
    return (tcoord, xcoord, flat_coord // depth_z, flat_coord % depth_z)


def block_colour(coords, t_offset, x_offset):
    return ((coords[0] + t_offset) // BLOCK + (coords[1] + x_offset) // BLOCK
            + coords[2] // BLOCK + coords[3] // BLOCK) % 2


def edge_masks(coords):
    return [(coords[direction] % BLOCK != BLOCK - 1, coords[direction] % BLOCK != 0) for direction in range(4)]


def dirac_local(vector, mats, keep_masks, depth_z):
    halves = project_all(vector)
    forward_list = []
    backward_list = []
    for direction in range(4):
        forward_term = colour_apply(mats[direction], neighbour(halves[2 * direction], direction, 1, depth_z))
        backward_term = neighbour(colour_adjoint(mats[direction], halves[2 * direction + 1]), direction, -1, depth_z)
        if keep_masks is not None:
            forward_term = jnp.where(keep_masks[direction][0], forward_term, 0.0)
            backward_term = jnp.where(keep_masks[direction][1], backward_term, 0.0)
        forward_list.append(forward_term)
        backward_list.append(backward_term)
    return combine(vector, forward_list, backward_list)


def coef_times(alpha_re, alpha_im, vector):
    split_pairs = vector.reshape((12, 2) + vector.shape[1:])
    real_part = split_pairs[:, 0]
    imag_part = split_pairs[:, 1]
    return jnp.stack([alpha_re * real_part - alpha_im * imag_part,
                      alpha_re * imag_part + alpha_im * real_part], axis=1).reshape(vector.shape)


def minimal_residual(residual, active, block_apply, block_total, block_spread):
    remainder = jnp.where(active, residual, 0.0)
    update = jnp.zeros_like(residual)
    for mr_step in range(MR_STEPS):
        applied = block_apply(remainder)
        pairs_applied = applied.reshape((12, 2) + applied.shape[1:])
        pairs_rest = remainder.reshape((12, 2) + remainder.shape[1:])
        applied_re, applied_im = pairs_applied[:, 0], pairs_applied[:, 1]
        rest_re, rest_im = pairs_rest[:, 0], pairs_rest[:, 1]
        block_stats = jnp.stack([jnp.sum(applied_re * rest_re + applied_im * rest_im, axis=0),
                                 jnp.sum(applied_re * rest_im - applied_im * rest_re, axis=0),
                                 jnp.sum(applied_re * applied_re + applied_im * applied_im, axis=0)])
        totals = block_total(block_stats)
        alpha_re = totals[0] / (totals[2] + DENOM_EPSILON)
        alpha_im = totals[1] / (totals[2] + DENOM_EPSILON)
        spread_vals = block_spread(jnp.stack([alpha_re, alpha_im]))
        update = update + coef_times(spread_vals[0], spread_vals[1], remainder)
        remainder = remainder - coef_times(spread_vals[0], spread_vals[1], applied)
    return update


def reference(source, gauge_links):
    site_shape = source.shape[1:]
    t_size, x_size, flat_size = site_shape
    mats = link_matrices(gauge_links)
    coords = site_coords(site_shape, LZ)
    colour = block_colour(coords, 0, 0)
    keep_masks = edge_masks(coords)
    t_blocks, x_blocks, y_blocks, z_blocks = t_size // BLOCK, x_size // BLOCK, LY // BLOCK, LZ // BLOCK

    def block_total(block_stats):
        grid_view = block_stats.reshape(block_stats.shape[0], t_blocks, BLOCK, x_blocks, BLOCK,
                                        y_blocks, BLOCK, z_blocks, BLOCK)
        return jnp.sum(grid_view, axis=(2, 4, 6, 8))

    def block_spread(block_values):
        rows_count = block_values.shape[0]
        expanded = jnp.broadcast_to(block_values[:, :, None, :, None, :, None, :, None],
                                    (rows_count, t_blocks, BLOCK, x_blocks, BLOCK, y_blocks, BLOCK, z_blocks, BLOCK))
        return expanded.reshape((rows_count,) + site_shape)

    def block_apply(vector):
        return dirac_local(vector, mats, keep_masks, LZ)

    solution = jnp.zeros_like(source)
    for cycle_index in range(CYCLES):
        for colour_now in range(2):
            residual = source - dirac_local(solution, mats, None, LZ)
            solution = solution + minimal_residual(residual, colour == colour_now, block_apply,
                                                   block_total, block_spread)
    residual = source - dirac_local(solution, mats, None, LZ)
    return solution, residual
```

```python
import jax
import jax.numpy as jnp
from jax import lax
from jax.experimental import pallas as pl
from jax.experimental.pallas import tpu as pltpu
from jax.sharding import PartitionSpec as P

MR_STEPS = 2
PERM = ((2, 3, 0, 1), (3, 2, 1, 0), (3, 2, 1, 0), (2, 3, 0, 1))
PHASE = (
    (1, 1, 1, 1),
    (1j, 1j, -1j, -1j),
    (-1, 1, 1, -1),
    (1j, -1j, -1j, 1j),
)
MASS_SHIFT = 4.1
DENOM_EPSILON = 1e-6
T, X, Y, Z = range(4)
MESH = pl.DeviceIdType.MESH


def lroll(v, shift):
    return pltpu.roll(v, shift % 128, 1)


def sroll(v, shift):
    shift %= 8
    return v if shift == 0 else pltpu.roll(v, shift, 0)


def plus_phase(x, phase, y):
    if phase == 1:
        return x[0] + y[0], x[1] + y[1]
    if phase == -1:
        return x[0] - y[0], x[1] - y[1]
    if phase == 1j:
        return x[0] - y[1], x[1] + y[0]
    return x[0] + y[1], x[1] - y[0]


def project(v, mu, parity):
    half = []
    for spin in (0, 1):
        phase, partner = parity * PHASE[mu][spin], PERM[mu][spin]
        for colour in range(3):
            at, other = 6 * spin + 2 * colour, 6 * partner + 2 * colour
            half += plus_phase((v[at], v[at + 1]), phase, (v[other], v[other + 1]))
    return half


def reconstruct(acc, half, mu, parity):
    acc = list(acc)
    for spin in range(4):
        phase, source = (1, spin) if spin < 2 else (parity * PHASE[mu][spin], PERM[mu][spin])
        for colour in range(3):
            at, other = 6 * spin + 2 * colour, 6 * source + 2 * colour
            acc[at], acc[at + 1] = plus_phase(
                (acc[at], acc[at + 1]), phase, (half[other], half[other + 1])
            )
    return acc


def times_link(link, half, adjoint):
    out = []
    entry = {}
    for spin in (0, 1):
        for row in range(3):
            re = im = None
            for col in range(3):
                key = 6 * col + 2 * row if adjoint else 6 * row + 2 * col
                if key not in entry:
                    entry[key] = link(key), link(key + 1)
                u_re, u_im = entry[key]
                h_re, h_im = half[6 * spin + 2 * col], half[6 * spin + 2 * col + 1]
                if adjoint:
                    re_term, im_term = u_re * h_re + u_im * h_im, u_re * h_im - u_im * h_re
                else:
                    re_term, im_term = u_re * h_re - u_im * h_im, u_re * h_im + u_im * h_re
                re = re_term if re is None else re + re_term
                im = im_term if im is None else im + im_term
            out += [re, im]
    return out


def kernel(
    counts, src_hbm, links_hbm, sol_hbm, res_hbm,
    src, links, raw, inner, rest, upd, app, sol, res, sent, got,
    in_sem, out_sem, send_sem, recv_sem,
):
    ta, gx = lax.axis_index("ta"), lax.axis_index("gx")
    n_ta, n_gx = counts
    sides = (
        {"ta": lax.rem(ta + n_ta - 1, n_ta)}, {"ta": lax.rem(ta + 1, n_ta)},
        {"gx": lax.rem(gx + n_gx - 1, n_gx)}, {"gx": lax.rem(gx + 1, n_gx)},
    )

    loads = [pltpu.make_async_copy(src_hbm, src, in_sem.at[4])]
    for mu in range(4):
        part = pl.ds(18 * mu, 18)
        loads.append(pltpu.make_async_copy(links_hbm.at[part], links.at[part], in_sem.at[mu]))
    for load in loads:
        load.start()
    barrier = pltpu.get_barrier_semaphore()
    for side in sides:
        pl.semaphore_signal(barrier, inc=1, device_id=side, device_id_type=MESH)

    row = lax.broadcasted_iota(jnp.int32, (8, 128), 0)
    lane = lax.broadcasted_iota(jnp.int32, (8, 128), 1)
    parity = lax.rem(ta + gx, 2)
    x, y, z = row % 4, (lane // 16) % 4, lane % 16
    t = 2 * (lane // 64) + row // 4
    first = (lane // 64 + z // 4 + parity) % 2 == 0
    low_lane, low_row = lane < 64, row < 4
    coords = (t, x, y, z % 4)
    inside = [jnp.where(coords[mu] == 3, 0.0, -0.5) for mu in range(4)]
    face_up = [jnp.where(coords[mu] == 3, 0.5, 0.0) for mu in range(4)]
    face_down = [jnp.where(coords[mu] == 0, 0.5, 0.0) for mu in range(4)]

    def pack(ref, k, colour):
        a, b = ref[k, 0:8, :], ref[k, 8:16, :]
        here = jnp.where(low_lane, a, b)
        there = lroll(jnp.where(low_lane, b, a), 64)
        return jnp.where(first, here, there) if colour == 0 else jnp.where(first, there, here)

    def unpack(ref, k, p0, p1):
        here = jnp.where(first, p0, p1)
        there = lroll(jnp.where(first, p1, p0), 64)
        ref[k, 0:8, :] = jnp.where(low_lane, here, there)
        ref[k, 8:16, :] = jnp.where(low_lane, there, here)

    def pack_links(mu, colour):
        for k in range(18 * mu, 18 * mu + 18):
            value = pack(links, k, colour)
            raw[colour, k] = value
            inner[colour, k] = value * inside[mu]

    def forward(v, mu):
        if mu == Z:
            return lroll(v, -1)
        if mu == Y:
            return lroll(v, -16)
        if mu == X:
            return sroll(v, -1)
        shifted = sroll(v, 4)
        return jnp.where(low_row, shifted, lroll(shifted, 64))

    def backward(v, mu):
        if mu == Z:
            return lroll(v, 1)
        if mu == Y:
            return lroll(v, 16)
        if mu == X:
            return sroll(v, 1)
        shifted = sroll(v, 4)
        return jnp.where(low_row, lroll(shifted, 64), shifted)

    def load(ref, colour):
        return [ref[colour, k] for k in range(24)]

    def block_apply(v, colour):
        acc = [MASS_SHIFT * value for value in v]
        for mu in range(4):
            link = lambda e, mu=mu: inner[colour, 18 * mu + e]
            half = [forward(h, mu) for h in project(v, mu, -1)]
            acc = reconstruct(acc, times_link(link, half, False), mu, -1)
            half = times_link(link, project(v, mu, 1), True)
            acc = reconstruct(acc, [backward(h, mu) for h in half], mu, 1)
        return acc

    def block_sum(v):
        for shift in (4, 2, 1):
            v = v + sroll(v, shift)
        for shift in (64, 32, 16):
            v = v + lroll(v, shift)
        v = v + jnp.where(lane % 2 == 0, lroll(v, -1), lroll(v, 1))
        return v + jnp.where(lane % 4 < 2, lroll(v, -2), lroll(v, 2))

    def minimal_residual(colour):
        for step in range(MR_STEPS):
            v = load(rest, colour)
            a = block_apply(v, colour)
            re = im = norm = None
            for k in range(0, 24, 2):
                a_re, a_im, v_re, v_im = a[k], a[k + 1], v[k], v[k + 1]
                terms = (
                    a_re * v_re + a_im * v_im, a_re * v_im - a_im * v_re, a_re * a_re + a_im * a_im
                )
                if k == 0:
                    re, im, norm = terms
                else:
                    re, im, norm = re + terms[0], im + terms[1], norm + terms[2]
                app[k], app[k + 1] = a_re, a_im
            re, im, norm = block_sum(re), block_sum(im), block_sum(norm)
            norm = norm + DENOM_EPSILON
            re, im = re / norm, im / norm
            for k in range(0, 24, 2):
                v_re, v_im = rest[colour, k], rest[colour, k + 1]
                a_re, a_im = app[k], app[k + 1]
                u_re, u_im = re * v_re - im * v_im, re * v_im + im * v_re
                if step > 0:
                    u_re, u_im = upd[colour, k] + u_re, upd[colour, k + 1] + u_im
                upd[colour, k], upd[colour, k + 1] = u_re, u_im
                rest[colour, k] = v_re - (re * a_re - im * a_im)
                rest[colour, k + 1] = v_im - (re * a_im + im * a_re)

    def squeeze_x(half, at):
        out = []
        for m in range(3):
            v = half[4 * m + at]
            for j in range(4):
                if j != at:
                    v = jnp.where(x == j, sroll(half[4 * m + j], j - at), v)
            out.append(v)
        return out

    def spread_x(three, to):
        return [sroll(three[k // 4], to - k % 4) for k in range(12)]

    def squeeze_t(half, high):
        rows = (row >= 4) if high else low_row
        lanes = (lane >= 64) if high else low_lane
        out = []
        for m in range(3):
            a, b, c, d = half[4 * m : 4 * m + 4]
            one = jnp.where(lanes, a, lroll(b, 64))
            two = jnp.where(lanes, c, lroll(d, 64))
            out.append(jnp.where(rows, one, sroll(two, 4)))
        return out

    def spread_t(three):
        out = []
        for v in three:
            s = sroll(v, 4)
            out += [lroll(s, 64), s, lroll(v, 64), v]
        return out

    def send_faces(colour, turn):
        u = load(upd, colour)
        copies = []
        for slot, (mu, up) in enumerate(((T, False), (T, True), (X, False), (X, True))):
            half = project(u, mu, 1 if up else -1)
            if up:
                half = times_link(lambda e, mu=mu: raw[colour, 18 * mu + e], half, True)
            three = squeeze_t(half, up) if mu == T else squeeze_x(half, 3 if up else 0)
            for m in range(3):
                sent[turn, slot, 8 * m : 8 * m + 8, :] = three[m]
            copy = pltpu.make_async_remote_copy(
                src_ref=sent.at[turn, slot],
                dst_ref=got.at[turn, slot],
                send_sem=send_sem.at[turn, slot],
                recv_sem=recv_sem.at[turn, slot],
                device_id=sides[slot],
                device_id_type=MESH,
            )
            copy.start()
            copies.append(copy)
        return copies

    def local_faces(colour, acc):
        u, other = load(upd, colour), 1 - colour
        for mu in (Y, Z):
            half = project(u, mu, -1)
            if mu == Y:
                half = [lroll(h, 48) for h in half]
            else:
                half = [jnp.where(z == 15, lroll(h, 15), lroll(h, -1)) for h in half]
            half = times_link(lambda e, mu=mu: raw[other, 18 * mu + e], half, False)
            acc = reconstruct(acc, [h * face_up[mu] for h in half], mu, -1)
            half = times_link(lambda e, mu=mu: raw[colour, 18 * mu + e], project(u, mu, 1), True)
            if mu == Y:
                half = [lroll(h, -48) for h in half]
            else:
                half = [jnp.where(z == 0, lroll(h, -15), lroll(h, 1)) for h in half]
            acc = reconstruct(acc, [h * face_down[mu] for h in half], mu, 1)
        return acc

    def far_faces(colour, turn, copies, acc):
        other = 1 - colour
        for slot, (mu, up) in enumerate(((T, False), (T, True), (X, False), (X, True))):
            copies[slot].wait()
            three = [got[turn, slot, 8 * m : 8 * m + 8, :] for m in range(3)]
            if up:
                half = spread_t(three) if mu == T else spread_x(three, 0)
                acc = reconstruct(acc, [h * face_down[mu] for h in half], mu, 1)
            else:
                half = spread_t(three) if mu == T else spread_x(three, 3)
                half = times_link(lambda e, mu=mu: raw[other, 18 * mu + e], half, False)
                acc = reconstruct(acc, [h * face_up[mu] for h in half], mu, -1)
        return acc

    loads[0].wait()
    for k in range(24):
        rest[0, k] = pack(src, k, 0)
    for mu in range(4):
        loads[1 + mu].wait()
        pack_links(mu, 0)
    minimal_residual(0)
    pl.semaphore_wait(barrier, 4)

    copies = send_faces(0, 0)
    for mu in range(4):
        pack_links(mu, 1)
    acc = local_faces(0, [pack(src, k, 1) for k in range(24)])
    acc = far_faces(0, 0, copies, acc)
    for k in range(24):
        rest[1, k] = acc[k]
    minimal_residual(1)

    copies = send_faces(1, 1)
    for k in range(24):
        unpack(sol, k, upd[0, k], upd[1, k])
    store_sol = pltpu.make_async_copy(sol, sol_hbm, out_sem.at[0])
    store_sol.start()
    acc = local_faces(1, load(rest, 0))
    acc = far_faces(1, 1, copies, acc)
    for k in range(24):
        unpack(res, k, acc[k], rest[1, k])
    store_res = pltpu.make_async_copy(res, res_hbm, out_sem.at[1])
    store_res.start()
    store_sol.wait()
    store_res.wait()


def solution(mesh):
    counts = mesh.shape["ta"], mesh.shape["gx"]

    def local(source, gauge_links):
        spinor = jax.ShapeDtypeStruct((24, 16, 128), jnp.float32)
        vmem = lambda *shape: pltpu.VMEM(shape, jnp.float32)
        out = pl.pallas_call(
            lambda *refs: kernel(counts, *refs),
            out_shape=(spinor, spinor),
            in_specs=[pl.BlockSpec(memory_space=pl.ANY)] * 2,
            out_specs=(pl.BlockSpec(memory_space=pl.ANY),) * 2,
            scratch_shapes=[
                vmem(24, 16, 128),
                vmem(72, 16, 128),
                vmem(2, 72, 8, 128),
                vmem(2, 72, 8, 128),
                vmem(2, 24, 8, 128),
                vmem(2, 24, 8, 128),
                vmem(24, 8, 128),
                vmem(24, 16, 128),
                vmem(24, 16, 128),
                vmem(2, 4, 24, 128),
                vmem(2, 4, 24, 128),
                pltpu.SemaphoreType.DMA((5,)),
                pltpu.SemaphoreType.DMA((2,)),
                pltpu.SemaphoreType.DMA((2, 4)),
                pltpu.SemaphoreType.DMA((2, 4)),
            ],
            compiler_params=pltpu.CompilerParams(
                collective_id=0, has_side_effects=True, vmem_limit_bytes=24 << 20
            ),
            name="schwarz",
        )(source.reshape(24, 16, 128), gauge_links.reshape(72, 16, 128))
        return tuple(value.reshape(24, 4, 4, 128) for value in out)

    return jax.shard_map(
        local,
        mesh=mesh,
        in_specs=(P(None, "ta", "gx", None), P(None, None, "ta", "gx", None)),
        out_specs=(P(None, "ta", "gx", None), P(None, "ta", "gx", None)),
        check_vma=False,
    )
```

```python
import jax
import jax.numpy as jnp
from jax import lax
from jax.experimental import pallas as pl
from jax.experimental.pallas import tpu as pltpu
from jax.sharding import PartitionSpec as P

MR_STEPS = 2
PERM = ((2, 3, 0, 1), (3, 2, 1, 0), (3, 2, 1, 0), (2, 3, 0, 1))
PHASE = (
    (1, 1, 1, 1),
    (1j, 1j, -1j, -1j),
    (-1, 1, 1, -1),
    (1j, -1j, -1j, 1j),
)
MASS_SHIFT = 4.1
DENOM_EPSILON = 1e-6
T, X, Y, Z = range(4)
MESH = pl.DeviceIdType.MESH


def lroll(v, shift):
    return pltpu.roll(v, shift % 128, 1)


def sroll(v, shift):
    shift %= 8
    return v if shift == 0 else pltpu.roll(v, shift, 0)


def plus_phase(x, phase, y):
    if phase == 1:
        return x[0] + y[0], x[1] + y[1]
    if phase == -1:
        return x[0] - y[0], x[1] - y[1]
    if phase == 1j:
        return x[0] - y[1], x[1] + y[0]
    return x[0] + y[1], x[1] - y[0]


def project(v, mu, parity):
    half = []
    for spin in (0, 1):
        phase, partner = parity * PHASE[mu][spin], PERM[mu][spin]
        for colour in range(3):
            at, other = 6 * spin + 2 * colour, 6 * partner + 2 * colour
            half += plus_phase((v[at], v[at + 1]), phase, (v[other], v[other + 1]))
    return half


def reconstruct(acc, half, mu, parity):
    acc = list(acc)
    for spin in range(4):
        phase, source = (1, spin) if spin < 2 else (parity * PHASE[mu][spin], PERM[mu][spin])
        for colour in range(3):
            at, other = 6 * spin + 2 * colour, 6 * source + 2 * colour
            acc[at], acc[at + 1] = plus_phase(
                (acc[at], acc[at + 1]), phase, (half[other], half[other + 1])
            )
    return acc


def times_link(link, half, adjoint):
    out = []
    entry = {}
    for spin in (0, 1):
        for row in range(3):
            re = im = None
            for col in range(3):
                key = 6 * col + 2 * row if adjoint else 6 * row + 2 * col
                if key not in entry:
                    entry[key] = link(key), link(key + 1)
                u_re, u_im = entry[key]
                h_re, h_im = half[6 * spin + 2 * col], half[6 * spin + 2 * col + 1]
                if adjoint:
                    re_term, im_term = u_re * h_re + u_im * h_im, u_re * h_im - u_im * h_re
                else:
                    re_term, im_term = u_re * h_re - u_im * h_im, u_re * h_im + u_im * h_re
                re = re_term if re is None else re + re_term
                im = im_term if im is None else im + im_term
            out += [re, im]
    return out


def first_colour(lane):
    parity = lax.rem(lax.axis_index("ta") + lax.axis_index("gx"), 2)
    return (lane // 64 + lane % 16 // 4 + parity) % 2 == 0


def store_kernel(upd, rest, sol_hbm, res_hbm, sol, res, out_sem):
    lane = lax.broadcasted_iota(jnp.int32, (8, 128), 1)
    first, low_lane = first_colour(lane), lane < 64
    stores = []
    for n, (packed, plain, out) in enumerate(((upd, sol, sol_hbm), (rest, res, res_hbm))):
        for k in range(24):
            p0, p1 = packed[0, k], packed[1, k]
            here = jnp.where(first, p0, p1)
            there = lroll(jnp.where(first, p1, p0), 64)
            plain[k, 0:8, :] = jnp.where(low_lane, here, there)
            plain[k, 8:16, :] = jnp.where(low_lane, there, here)
        store = pltpu.make_async_copy(plain, out, out_sem.at[n])
        store.start()
        stores.append(store)
    for store in stores:
        store.wait()


def kernel(
    counts, src_hbm, links_hbm, upd, rest,
    src, links, raw, inner, app, sent, got, in_sem, send_sem, recv_sem,
):
    ta, gx = lax.axis_index("ta"), lax.axis_index("gx")
    n_ta, n_gx = counts
    sides = (
        {"ta": lax.rem(ta + n_ta - 1, n_ta)}, {"ta": lax.rem(ta + 1, n_ta)},
        {"gx": lax.rem(gx + n_gx - 1, n_gx)}, {"gx": lax.rem(gx + 1, n_gx)},
    )

    loads = [pltpu.make_async_copy(src_hbm, src, in_sem.at[4])]
    for mu in range(4):
        part = pl.ds(18 * mu, 18)
        loads.append(pltpu.make_async_copy(links_hbm.at[part], links.at[part], in_sem.at[mu]))
    for load in loads:
        load.start()
    barrier = pltpu.get_barrier_semaphore()
    for side in sides:
        pl.semaphore_signal(barrier, inc=1, device_id=side, device_id_type=MESH)

    row = lax.broadcasted_iota(jnp.int32, (8, 128), 0)
    lane = lax.broadcasted_iota(jnp.int32, (8, 128), 1)
    x, y, z = row % 4, (lane // 16) % 4, lane % 16
    t = 2 * (lane // 64) + row // 4
    first = first_colour(lane)
    low_lane, low_row = lane < 64, row < 4
    coords = (t, x, y, z % 4)
    inside = [jnp.where(coords[mu] == 3, 0.0, -0.5) for mu in range(4)]
    face_up = [jnp.where(coords[mu] == 3, 0.5, 0.0) for mu in range(4)]
    face_down = [jnp.where(coords[mu] == 0, 0.5, 0.0) for mu in range(4)]

    def pack(ref, k, colour):
        a, b = ref[k, 0:8, :], ref[k, 8:16, :]
        here = jnp.where(low_lane, a, b)
        there = lroll(jnp.where(low_lane, b, a), 64)
        return jnp.where(first, here, there) if colour == 0 else jnp.where(first, there, here)

    def pack_links(mu, colour):
        for k in range(18 * mu, 18 * mu + 18):
            value = pack(links, k, colour)
            raw[colour, k] = value
            inner[colour, k] = value * inside[mu]

    def forward(v, mu):
        if mu == Z:
            return lroll(v, -1)
        if mu == Y:
            return lroll(v, -16)
        if mu == X:
            return sroll(v, -1)
        shifted = sroll(v, 4)
        return jnp.where(low_row, shifted, lroll(shifted, 64))

    def backward(v, mu):
        if mu == Z:
            return lroll(v, 1)
        if mu == Y:
            return lroll(v, 16)
        if mu == X:
            return sroll(v, 1)
        shifted = sroll(v, 4)
        return jnp.where(low_row, lroll(shifted, 64), shifted)

    def load(ref, colour):
        return [ref[colour, k] for k in range(24)]

    def block_apply(v, colour):
        acc = [MASS_SHIFT * value for value in v]
        for mu in range(4):
            link = lambda e, mu=mu: inner[colour, 18 * mu + e]
            half = [forward(h, mu) for h in project(v, mu, -1)]
            acc = reconstruct(acc, times_link(link, half, False), mu, -1)
            half = times_link(link, project(v, mu, 1), True)
            acc = reconstruct(acc, [backward(h, mu) for h in half], mu, 1)
        return acc

    def block_sum(v):
        for shift in (4, 2, 1):
            v = v + sroll(v, shift)
        for shift in (64, 32, 16):
            v = v + lroll(v, shift)
        v = v + jnp.where(lane % 2 == 0, lroll(v, -1), lroll(v, 1))
        return v + jnp.where(lane % 4 < 2, lroll(v, -2), lroll(v, 2))

    def minimal_residual(colour):
        for step in range(MR_STEPS):
            v = load(rest, colour)
            a = block_apply(v, colour)
            re = im = norm = None
            for k in range(0, 24, 2):
                a_re, a_im, v_re, v_im = a[k], a[k + 1], v[k], v[k + 1]
                terms = (
                    a_re * v_re + a_im * v_im, a_re * v_im - a_im * v_re, a_re * a_re + a_im * a_im
                )
                if k == 0:
                    re, im, norm = terms
                else:
                    re, im, norm = re + terms[0], im + terms[1], norm + terms[2]
                app[k], app[k + 1] = a_re, a_im
            re, im, norm = block_sum(re), block_sum(im), block_sum(norm)
            norm = norm + DENOM_EPSILON
            re, im = re / norm, im / norm
            for k in range(0, 24, 2):
                v_re, v_im = rest[colour, k], rest[colour, k + 1]
                a_re, a_im = app[k], app[k + 1]
                u_re, u_im = re * v_re - im * v_im, re * v_im + im * v_re
                if step > 0:
                    u_re, u_im = upd[colour, k] + u_re, upd[colour, k + 1] + u_im
                upd[colour, k], upd[colour, k + 1] = u_re, u_im
                rest[colour, k] = v_re - (re * a_re - im * a_im)
                rest[colour, k + 1] = v_im - (re * a_im + im * a_re)

    def squeeze_x(half, at):
        out = []
        for m in range(3):
            v = half[4 * m + at]
            for j in range(4):
                if j != at:
                    v = jnp.where(x == j, sroll(half[4 * m + j], j - at), v)
            out.append(v)
        return out

    def spread_x(three, to):
        return [sroll(three[k // 4], to - k % 4) for k in range(12)]

    def squeeze_t(half, high):
        rows = (row >= 4) if high else low_row
        lanes = (lane >= 64) if high else low_lane
        out = []
        for m in range(3):
            a, b, c, d = half[4 * m : 4 * m + 4]
            one = jnp.where(lanes, a, lroll(b, 64))
            two = jnp.where(lanes, c, lroll(d, 64))
            out.append(jnp.where(rows, one, sroll(two, 4)))
        return out

    def spread_t(three):
        out = []
        for v in three:
            s = sroll(v, 4)
            out += [lroll(s, 64), s, lroll(v, 64), v]
        return out

    def send_faces(colour, turn):
        u = load(upd, colour)
        copies = []
        for slot, (mu, up) in enumerate(((T, False), (T, True), (X, False), (X, True))):
            half = project(u, mu, 1 if up else -1)
            if up:
                half = times_link(lambda e, mu=mu: raw[colour, 18 * mu + e], half, True)
            three = squeeze_t(half, up) if mu == T else squeeze_x(half, 3 if up else 0)
            for m in range(3):
                sent[turn, slot, 8 * m : 8 * m + 8, :] = three[m]
            copy = pltpu.make_async_remote_copy(
                src_ref=sent.at[turn, slot],
                dst_ref=got.at[turn, slot],
                send_sem=send_sem.at[turn, slot],
                recv_sem=recv_sem.at[turn, slot],
                device_id=sides[slot],
                device_id_type=MESH,
            )
            copy.start()
            copies.append(copy)
        return copies

    def local_faces(colour, acc):
        u, other = load(upd, colour), 1 - colour
        for mu in (Y, Z):
            half = project(u, mu, -1)
            if mu == Y:
                half = [lroll(h, 48) for h in half]
            else:
                half = [jnp.where(z == 15, lroll(h, 15), lroll(h, -1)) for h in half]
            half = times_link(lambda e, mu=mu: raw[other, 18 * mu + e], half, False)
            acc = reconstruct(acc, [h * face_up[mu] for h in half], mu, -1)
            half = times_link(lambda e, mu=mu: raw[colour, 18 * mu + e], project(u, mu, 1), True)
            if mu == Y:
                half = [lroll(h, -48) for h in half]
            else:
                half = [jnp.where(z == 0, lroll(h, -15), lroll(h, 1)) for h in half]
            acc = reconstruct(acc, [h * face_down[mu] for h in half], mu, 1)
        return acc

    def far_faces(colour, turn, copies, acc):
        other = 1 - colour
        for slot, (mu, up) in enumerate(((T, False), (T, True), (X, False), (X, True))):
            copies[slot].wait()
            three = [got[turn, slot, 8 * m : 8 * m + 8, :] for m in range(3)]
            if up:
                half = spread_t(three) if mu == T else spread_x(three, 0)
                acc = reconstruct(acc, [h * face_down[mu] for h in half], mu, 1)
            else:
                half = spread_t(three) if mu == T else spread_x(three, 3)
                half = times_link(lambda e, mu=mu: raw[other, 18 * mu + e], half, False)
                acc = reconstruct(acc, [h * face_up[mu] for h in half], mu, -1)
        return acc

    loads[0].wait()
    for k in range(24):
        rest[0, k] = pack(src, k, 0)
    for mu in range(4):
        loads[1 + mu].wait()
        pack_links(mu, 0)
    minimal_residual(0)
    pl.semaphore_wait(barrier, 4)

    copies = send_faces(0, 0)
    for mu in range(4):
        pack_links(mu, 1)
    acc = local_faces(0, [pack(src, k, 1) for k in range(24)])
    acc = far_faces(0, 0, copies, acc)
    for k in range(24):
        rest[1, k] = acc[k]
    minimal_residual(1)

    copies = send_faces(1, 1)
    acc = local_faces(1, load(rest, 0))
    acc = far_faces(1, 1, copies, acc)
    for k in range(24):
        rest[0, k] = acc[k]


def solution(mesh):
    counts = mesh.shape["ta"], mesh.shape["gx"]

    def local(source, gauge_links):
        spinor = pltpu.HBM((24, 16, 128), jnp.float32)
        vmem = lambda *shape: pltpu.VMEM(shape, jnp.float32)
        packed = pltpu.VMEM((2, 24, 8, 128), jnp.float32)
        hbm, in_vmem = pl.BlockSpec(memory_space=pltpu.HBM), pl.BlockSpec(memory_space=pltpu.VMEM)
        upd, rest = pl.pallas_call(
            lambda *refs: kernel(counts, *refs),
            out_shape=(packed, packed),
            in_specs=[hbm, hbm],
            out_specs=(in_vmem, in_vmem),
            scratch_shapes=[
                vmem(24, 16, 128),
                vmem(72, 16, 128),
                vmem(2, 72, 8, 128),
                vmem(2, 72, 8, 128),
                vmem(24, 8, 128),
                vmem(2, 4, 24, 128),
                vmem(2, 4, 24, 128),
                pltpu.SemaphoreType.DMA((5,)),
                pltpu.SemaphoreType.DMA((2, 4)),
                pltpu.SemaphoreType.DMA((2, 4)),
            ],
            compiler_params=pltpu.CompilerParams(
                collective_id=0, has_side_effects=True, vmem_limit_bytes=24 << 20
            ),
            name="schwarz",
        )(
            pltpu.with_memory_space_constraint(source.reshape(24, 16, 128), pltpu.HBM),
            pltpu.with_memory_space_constraint(gauge_links.reshape(72, 16, 128), pltpu.HBM),
        )
        out = pl.pallas_call(
            store_kernel,
            out_shape=(spinor, spinor),
            in_specs=[in_vmem, in_vmem],
            out_specs=(hbm, hbm),
            scratch_shapes=[
                vmem(24, 16, 128), vmem(24, 16, 128), pltpu.SemaphoreType.DMA((2,)),
            ],
            compiler_params=pltpu.CompilerParams(vmem_limit_bytes=4 << 20),
            name="store",
        )(
            pltpu.with_memory_space_constraint(upd, pltpu.VMEM),
            pltpu.with_memory_space_constraint(rest, pltpu.VMEM),
        )
        return tuple(value.reshape(24, 4, 4, 128) for value in out)

    return jax.shard_map(
        local,
        mesh=mesh,
        in_specs=(P(None, "ta", "gx", None), P(None, None, "ta", "gx", None)),
        out_specs=(P(None, "ta", "gx", None), P(None, "ta", "gx", None)),
        check_vma=False,
    )
```

```python
import jax
import jax.numpy as jnp
from jax import lax
from jax.experimental import pallas as pl
from jax.experimental.pallas import tpu as pltpu
from jax.sharding import PartitionSpec as P

MR_STEPS = 2
PERM = ((2, 3, 0, 1), (3, 2, 1, 0), (3, 2, 1, 0), (2, 3, 0, 1))
PHASE = (
    (1, 1, 1, 1),
    (1j, 1j, -1j, -1j),
    (-1, 1, 1, -1),
    (1j, -1j, -1j, 1j),
)
MASS_SHIFT = 4.1
DENOM_EPSILON = 1e-6
T, X, Y, Z = range(4)
MESH = pl.DeviceIdType.MESH


def lroll(v, shift):
    return pltpu.roll(v, shift % 128, 1)


def sroll(v, shift):
    shift %= 8
    return v if shift == 0 else pltpu.roll(v, shift, 0)


def plus_phase(x, phase, y):
    if phase == 1:
        return x[0] + y[0], x[1] + y[1]
    if phase == -1:
        return x[0] - y[0], x[1] - y[1]
    if phase == 1j:
        return x[0] - y[1], x[1] + y[0]
    return x[0] + y[1], x[1] - y[0]


def project(v, mu, parity):
    half = []
    for spin in (0, 1):
        phase, partner = parity * PHASE[mu][spin], PERM[mu][spin]
        for colour in range(3):
            at, other = 6 * spin + 2 * colour, 6 * partner + 2 * colour
            half += plus_phase((v[at], v[at + 1]), phase, (v[other], v[other + 1]))
    return half


def reconstruct(acc, half, mu, parity):
    acc = list(acc)
    for spin in range(4):
        phase, source = (1, spin) if spin < 2 else (parity * PHASE[mu][spin], PERM[mu][spin])
        for colour in range(3):
            at, other = 6 * spin + 2 * colour, 6 * source + 2 * colour
            acc[at], acc[at + 1] = plus_phase(
                (acc[at], acc[at + 1]), phase, (half[other], half[other + 1])
            )
    return acc


def times_link(link, half, adjoint):
    out = []
    entry = {}
    for spin in (0, 1):
        for row in range(3):
            re = im = None
            for col in range(3):
                key = 6 * col + 2 * row if adjoint else 6 * row + 2 * col
                if key not in entry:
                    entry[key] = link(key), link(key + 1)
                u_re, u_im = entry[key]
                h_re, h_im = half[6 * spin + 2 * col], half[6 * spin + 2 * col + 1]
                if adjoint:
                    re_term, im_term = u_re * h_re + u_im * h_im, u_re * h_im - u_im * h_re
                else:
                    re_term, im_term = u_re * h_re - u_im * h_im, u_re * h_im + u_im * h_re
                re = re_term if re is None else re + re_term
                im = im_term if im is None else im + im_term
            out += [re, im]
    return out


def store_kernel(sol, res, sol_hbm, res_hbm, out_sem):
    stores = (
        pltpu.make_async_copy(sol, sol_hbm, out_sem.at[0]),
        pltpu.make_async_copy(res, res_hbm, out_sem.at[1]),
    )
    for store in stores:
        store.start()
    for store in stores:
        store.wait()


def times_link_by_three(link, half, adjoint):
    entry = {}
    sums = [half[n] + half[n + 1] for n in range(0, 12, 2)]
    out = []
    for spin in (0, 1):
        for row in range(3):
            one = two = three = None
            for col in range(3):
                key = (col, row) if adjoint else (row, col)
                if key not in entry:
                    entry[key] = link(3 * key[0] + key[1])
                u_re, u_plus, u_minus = entry[key]
                h_re, h_im = half[6 * spin + 2 * col], half[6 * spin + 2 * col + 1]
                if adjoint:
                    terms = u_re * sums[3 * spin + col], u_plus * h_re, u_minus * h_im
                else:
                    terms = u_re * sums[3 * spin + col], u_minus * h_re, u_plus * h_im
                if col == 0:
                    one, two, three = terms
                else:
                    one, two, three = one + terms[0], two + terms[1], three + terms[2]
            out += [one + three, one - two] if adjoint else [one - three, one + two]
    return out


def kernel(
    counts, src_hbm, links_hbm, sol, res,
    src, links, raw, inner, upd, rest, app, sent, got, in_sem, send_sem, recv_sem,
):
    ta, gx = lax.axis_index("ta"), lax.axis_index("gx")
    n_ta, n_gx = counts
    sides = (
        {"ta": lax.rem(ta + n_ta - 1, n_ta)}, {"ta": lax.rem(ta + 1, n_ta)},
        {"gx": lax.rem(gx + n_gx - 1, n_gx)}, {"gx": lax.rem(gx + 1, n_gx)},
    )

    barrier = pltpu.get_barrier_semaphore()
    for side in sides:
        pl.semaphore_signal(barrier, inc=1, device_id=side, device_id_type=MESH)
    loads = [pltpu.make_async_copy(src_hbm, src, in_sem.at[4])]
    for mu in range(4):
        part = pl.ds(18 * mu, 18)
        loads.append(pltpu.make_async_copy(links_hbm.at[part], links.at[part], in_sem.at[mu]))
    for load in loads:
        load.start()

    row = lax.broadcasted_iota(jnp.int32, (8, 128), 0)
    lane = lax.broadcasted_iota(jnp.int32, (8, 128), 1)
    x, y, z = row % 4, (lane // 16) % 4, lane % 16
    t = 2 * (lane // 64) + row // 4
    first = (lane // 64 + z // 4 + lax.rem(ta + gx, 2)) % 2 == 0
    low_lane, low_row = lane < 64, row < 4
    coords = (t, x, y, z % 4)
    lane_row = lax.broadcasted_iota(jnp.int32, (128, 128), 0)
    lane_col = lax.broadcasted_iota(jnp.int32, (128, 128), 1)
    same_block = (lane_row % 16 // 4 == lane_col % 16 // 4).astype(jnp.bfloat16)
    inside = [jnp.where(coords[mu] == 3, 0.0, -0.5 / MASS_SHIFT) for mu in range(4)]
    face_up = [jnp.where(coords[mu] == 3, 0.5, 0.0) for mu in range(4)]
    face_down = [jnp.where(coords[mu] == 0, 0.5, 0.0) for mu in range(4)]

    def pack(ref, k, colour):
        a, b = ref[k, 0:8, :], ref[k, 8:16, :]
        here = jnp.where(low_lane, a, b)
        there = lroll(jnp.where(low_lane, b, a), 64)
        return jnp.where(first, here, there) if colour == 0 else jnp.where(first, there, here)

    def unpack(ref, k, p0, p1):
        here = jnp.where(first, p0, p1)
        there = lroll(jnp.where(first, p1, p0), 64)
        ref[k, 0:8, :] = jnp.where(low_lane, here, there)
        ref[k, 8:16, :] = jnp.where(low_lane, there, here)

    def pack_links(mu, colour):
        for k in range(9 * mu, 9 * mu + 9):
            re, im = pack(links, 2 * k, colour), pack(links, 2 * k + 1, colour)
            raw[colour, 2 * k], raw[colour, 2 * k + 1] = re, im
            re, im = re * inside[mu], im * inside[mu]
            inner[colour, 3 * k] = re
            inner[colour, 3 * k + 1] = im + re
            inner[colour, 3 * k + 2] = im - re

    def forward(v, mu):
        if mu == Z:
            return lroll(v, -1)
        if mu == Y:
            return lroll(v, -16)
        if mu == X:
            return sroll(v, -1)
        shifted = sroll(v, 4)
        return jnp.where(low_row, shifted, lroll(shifted, 64))

    def backward(v, mu):
        if mu == Z:
            return lroll(v, 1)
        if mu == Y:
            return lroll(v, 16)
        if mu == X:
            return sroll(v, 1)
        shifted = sroll(v, 4)
        return jnp.where(low_row, lroll(shifted, 64), shifted)

    def load(ref, colour):
        return [ref[colour, k] for k in range(24)]

    def store(ref, colour, values):
        for k in range(24):
            ref[colour, k] = values[k]

    def block_apply(v, colour):
        acc = v
        for mu in range(4):
            link = lambda e, mu=mu: [inner[colour, 27 * mu + 3 * e + n] for n in range(3)]
            half = [forward(h, mu) for h in project(v, mu, -1)]
            acc = reconstruct(acc, times_link_by_three(link, half, False), mu, -1)
            half = times_link_by_three(link, project(v, mu, 1), True)
            acc = reconstruct(acc, [backward(h, mu) for h in half], mu, 1)
        return acc

    def block_sums(stats):
        for shift in (4, 2, 1):
            stats = [v + sroll(v, shift) for v in stats]
        rows = jnp.where(row == 0, stats[0], jnp.where(row == 1, stats[1], stats[2]))
        pieces = []
        for _ in range(3):
            pieces.append(rows.astype(jnp.bfloat16).astype(jnp.float32))
            rows = rows - pieces[-1]
        pieces.append(jnp.zeros_like(rows))
        split = jnp.concatenate(pieces).astype(jnp.bfloat16)
        sums = jnp.dot(split, same_block, preferred_element_type=jnp.float32)
        sums = sums[0:8] + sums[8:16] + sums[16:24]
        return [jnp.broadcast_to(sums[n : n + 1], (8, 128)) for n in range(3)]

    def coefficient(a, v):
        re = im = norm = None
        for k in range(0, 24, 2):
            a_re, a_im, v_re, v_im = a[k], a[k + 1], v[k], v[k + 1]
            terms = a_re * v_re + a_im * v_im, a_re * v_im - a_im * v_re, a_re * a_re + a_im * a_im
            if k == 0:
                re, im, norm = terms
            else:
                re, im, norm = re + terms[0], im + terms[1], norm + terms[2]
        re, im, norm = block_sums([re, im, norm])
        norm = norm + DENOM_EPSILON / MASS_SHIFT**2
        alpha = re / norm, im / norm
        return alpha, [value * (1 / MASS_SHIFT) for value in alpha]

    def plus_times(x, sign, alpha, y):
        out = []
        for k in range(0, 24, 2):
            re = alpha[0] * y[k] - alpha[1] * y[k + 1]
            im = alpha[0] * y[k + 1] + alpha[1] * y[k]
            if x is None:
                out += [re, im]
            elif sign > 0:
                out += [x[k] + re, x[k + 1] + im]
            else:
                out += [x[k] - re, x[k + 1] - im]
        return out

    def minimal_residual(colour):
        v = load(rest, colour)
        a = block_apply(v, colour)
        store(app, 0, a)
        b = block_apply(a, colour)
        alpha, scaled = coefficient(a, v)
        v, a = load(rest, colour), load(app, 0)
        update = plus_times(None, 1, scaled, v)
        v = plus_times(v, -1, alpha, a)
        a = plus_times(a, -1, alpha, b)
        store(app, 0, a)
        store(rest, colour, v)
        alpha, scaled = coefficient(a, v)
        update = plus_times(update, 1, scaled, load(rest, colour))
        store(upd, colour, update)
        return update, alpha

    def squeeze_x(half, at):
        out = []
        for m in range(3):
            v = half[4 * m + at]
            for j in range(4):
                if j != at:
                    v = jnp.where(x == j, sroll(half[4 * m + j], j - at), v)
            out.append(v)
        return out

    def spread_x(three, to):
        return [sroll(three[k // 4], to - k % 4) for k in range(12)]

    def squeeze_t(half, high):
        rows = (row >= 4) if high else low_row
        lanes = (lane >= 64) if high else low_lane
        out = []
        for m in range(3):
            a, b, c, d = half[4 * m : 4 * m + 4]
            one = jnp.where(lanes, a, lroll(b, 64))
            two = jnp.where(lanes, c, lroll(d, 64))
            out.append(jnp.where(rows, one, sroll(two, 4)))
        return out

    def spread_t(three):
        out = []
        for v in three:
            s = sroll(v, 4)
            out += [lroll(s, 64), s, lroll(v, 64), v]
        return out

    def faces(u, colour, slot):
        mu, up = slot // 2, slot % 2 == 1
        half = project(u, mu, 1 if up else -1)
        if up:
            half = times_link(lambda e: raw[colour, 18 * mu + e], half, True)
        three = squeeze_t(half, up) if mu == T else squeeze_x(half, 3 if up else 0)
        for m in range(3):
            sent[colour, slot, 8 * m : 8 * m + 8, :] = three[m]

    def send(colour, slots):
        @pl.when(ta >= 0)
        def _():
            for slot in slots:
                pltpu.make_async_remote_copy(
                    src_ref=sent.at[colour, slot],
                    dst_ref=got.at[colour, slot],
                    send_sem=send_sem.at[0],
                    recv_sem=recv_sem.at[colour, min(slot, 2)],
                    device_id=sides[slot],
                    device_id_type=MESH,
                ).start()

    def await_face(colour, slot, count=1):
        part = got.at[colour, pl.ds(slot, count)]
        pltpu.make_async_copy(part, part, recv_sem.at[colour, slot]).wait()

    def local_faces(u, colour, acc):
        other = 1 - colour
        for mu in (Y, Z):
            half = project(u, mu, -1)
            if mu == Y:
                half = [lroll(h, 48) for h in half]
            else:
                half = [jnp.where(z == 15, lroll(h, 15), lroll(h, -1)) for h in half]
            half = times_link(lambda e, mu=mu: raw[other, 18 * mu + e], half, False)
            acc = reconstruct(acc, [h * face_up[mu] for h in half], mu, -1)
            half = times_link(lambda e, mu=mu: raw[colour, 18 * mu + e], project(u, mu, 1), True)
            if mu == Y:
                half = [lroll(h, -48) for h in half]
            else:
                half = [jnp.where(z == 0, lroll(h, -15), lroll(h, 1)) for h in half]
            acc = reconstruct(acc, [h * face_down[mu] for h in half], mu, 1)
        return acc

    def add_face(acc, colour, slot):
        mu, up = slot // 2, slot % 2 == 1
        three = [got[colour, slot, 8 * m : 8 * m + 8, :] for m in range(3)]
        if up:
            half = spread_t(three) if mu == T else spread_x(three, 0)
            return reconstruct(acc, [h * face_down[mu] for h in half], mu, 1)
        half = spread_t(three) if mu == T else spread_x(three, 3)
        half = times_link(lambda e: raw[1 - colour, 18 * mu + e], half, False)
        return reconstruct(acc, [h * face_up[mu] for h in half], mu, -1)

    loads[0].wait()
    for k in range(24):
        rest[0, k] = pack(src, k, 0)
    for mu in range(4):
        loads[1 + mu].wait()
    for mu in range(4):
        pack_links(mu, 0)

    update, alpha = minimal_residual(0)
    for slot in range(4):
        faces(update, 0, slot)
    pl.semaphore_wait(barrier, 4)
    send(0, (0, 1, 2, 3))
    for k in range(24):
        rest[1, k] = pack(src, k, 1)
    for mu in range(4):
        pack_links(mu, 1)
    store(rest, 0, plus_times(load(rest, 0), -1, alpha, load(app, 0)))
    acc = local_faces(load(upd, 0), 0, load(rest, 1))
    store(rest, 1, acc)
    await_face(0, 2, 2)
    acc = add_face(add_face(load(rest, 1), 0, 2), 0, 3)
    store(rest, 1, acc)
    await_face(0, 1)
    await_face(0, 0)
    store(rest, 1, add_face(add_face(load(rest, 1), 0, 1), 0, 0))

    update, alpha = minimal_residual(1)
    faces(update, 1, 1)
    send(1, (1,))
    faces(update, 1, 3)
    send(1, (3,))
    for slot in (2, 0):
        faces(update, 1, slot)
    send(1, (2, 0))
    store(rest, 1, plus_times(load(rest, 1), -1, alpha, load(app, 0)))
    for k in range(24):
        unpack(sol, k, upd[0, k], upd[1, k])
    store(rest, 0, local_faces(load(upd, 1), 1, load(rest, 0)))
    await_face(1, 2, 2)
    store(rest, 0, add_face(add_face(load(rest, 0), 1, 2), 1, 3))
    await_face(1, 0)
    acc = add_face(load(rest, 0), 1, 0)
    for k in range(24):
        unpack(res, k, acc[k], rest[1, k])
    pltpu.make_async_copy(sent, sent, send_sem.at[0]).wait()
    at_zero = jnp.where(first & low_row, 0.5, 0.0)
    await_face(1, 1)
    half = []
    for m in range(3):
        v = got[1, 1, 8 * m : 8 * m + 8, :]
        s = sroll(v, 4)
        v_far, s_far = lroll(v, 64), lroll(s, 64)
        half += [
            jnp.where(low_lane, s_far, s), jnp.where(low_lane, s, s_far),
            jnp.where(low_lane, v_far, v), jnp.where(low_lane, v, v_far),
        ]
    acc = [res[k, 0:8, :] for k in range(24)]
    acc = reconstruct(acc, [h * at_zero for h in half], T, 1)
    for k in range(24):
        res[k, 0:8, :] = acc[k]


def solution(mesh):
    counts = mesh.shape["ta"], mesh.shape["gx"]

    def local(source, gauge_links):
        spinor = pltpu.HBM((24, 16, 128), jnp.float32)
        vmem = lambda *shape: pltpu.VMEM(shape, jnp.float32)
        plain = pltpu.VMEM((24, 16, 128), jnp.float32)
        hbm, in_vmem = pl.BlockSpec(memory_space=pltpu.HBM), pl.BlockSpec(memory_space=pltpu.VMEM)
        out = pl.pallas_call(
            lambda *refs: kernel(counts, *refs),
            out_shape=(plain, plain),
            in_specs=[hbm, hbm],
            out_specs=(in_vmem, in_vmem),
            scratch_shapes=[
                vmem(24, 16, 128),
                vmem(72, 16, 128),
                vmem(2, 72, 8, 128),
                vmem(2, 108, 8, 128),
                vmem(2, 24, 8, 128),
                vmem(2, 24, 8, 128),
                vmem(1, 24, 8, 128),
                vmem(2, 4, 24, 128),
                vmem(2, 4, 24, 128),
                pltpu.SemaphoreType.DMA((5,)),
                pltpu.SemaphoreType.DMA((1,)),
                pltpu.SemaphoreType.DMA((2, 3)),
            ],
            compiler_params=pltpu.CompilerParams(
                collective_id=0, has_side_effects=True, vmem_limit_bytes=24 << 20
            ),
            name="schwarz",
        )(
            pltpu.with_memory_space_constraint(source.reshape(24, 16, 128), pltpu.HBM),
            pltpu.with_memory_space_constraint(gauge_links.reshape(72, 16, 128), pltpu.HBM),
        )
        out = pl.pallas_call(
            store_kernel,
            out_shape=(spinor, spinor),
            in_specs=[in_vmem, in_vmem],
            out_specs=(hbm, hbm),
            scratch_shapes=[pltpu.SemaphoreType.DMA((2,))],
            compiler_params=pltpu.CompilerParams(vmem_limit_bytes=4 << 20),
            name="store",
        )(*(pltpu.with_memory_space_constraint(value, pltpu.VMEM) for value in out))
        return tuple(value.reshape(24, 4, 4, 128) for value in out)

    return jax.shard_map(
        local,
        mesh=mesh,
        in_specs=(P(None, "ta", "gx", None), P(None, None, "ta", "gx", None)),
        out_specs=(P(None, "ta", "gx", None), P(None, "ta", "gx", None)),
        check_vma=False,
    )
```

```python
import jax
import jax.numpy as jnp
from jax import lax
from jax.experimental import pallas as pl
from jax.experimental.pallas import tpu as pltpu
from jax.sharding import PartitionSpec as P

MR_STEPS = 2
PERM = ((2, 3, 0, 1), (3, 2, 1, 0), (3, 2, 1, 0), (2, 3, 0, 1))
PHASE = (
    (1, 1, 1, 1),
    (1j, 1j, -1j, -1j),
    (-1, 1, 1, -1),
    (1j, -1j, -1j, 1j),
)
MASS_SHIFT = 4.1
DENOM_EPSILON = 1e-6
T, X, Y, Z = range(4)
MESH = pl.DeviceIdType.MESH


def lroll(v, shift):
    return pltpu.roll(v, shift % 128, 1)


def sroll(v, shift):
    shift %= 8
    return v if shift == 0 else pltpu.roll(v, shift, 0)


def plus_phase(x, phase, y):
    if phase == 1:
        return x[0] + y[0], x[1] + y[1]
    if phase == -1:
        return x[0] - y[0], x[1] - y[1]
    if phase == 1j:
        return x[0] - y[1], x[1] + y[0]
    return x[0] + y[1], x[1] - y[0]


def project(v, mu, parity):
    half = []
    for spin in (0, 1):
        phase, partner = parity * PHASE[mu][spin], PERM[mu][spin]
        for colour in range(3):
            at, other = 6 * spin + 2 * colour, 6 * partner + 2 * colour
            half += plus_phase((v[at], v[at + 1]), phase, (v[other], v[other + 1]))
    return half


def reconstruct(acc, half, mu, parity):
    acc = list(acc)
    for spin in range(4):
        phase, source = (1, spin) if spin < 2 else (parity * PHASE[mu][spin], PERM[mu][spin])
        for colour in range(3):
            at, other = 6 * spin + 2 * colour, 6 * source + 2 * colour
            acc[at], acc[at + 1] = plus_phase(
                (acc[at], acc[at + 1]), phase, (half[other], half[other + 1])
            )
    return acc


def times_link(link, half, adjoint):
    out = []
    entry = {}
    for spin in (0, 1):
        for row in range(3):
            re = im = None
            for col in range(3):
                key = 6 * col + 2 * row if adjoint else 6 * row + 2 * col
                if key not in entry:
                    entry[key] = link(key), link(key + 1)
                u_re, u_im = entry[key]
                h_re, h_im = half[6 * spin + 2 * col], half[6 * spin + 2 * col + 1]
                if adjoint:
                    re_term, im_term = u_re * h_re + u_im * h_im, u_re * h_im - u_im * h_re
                else:
                    re_term, im_term = u_re * h_re - u_im * h_im, u_re * h_im + u_im * h_re
                re = re_term if re is None else re + re_term
                im = im_term if im is None else im + im_term
            out += [re, im]
    return out


def store_kernel(sol, res, sol_hbm, res_hbm, out_sem):
    stores = (
        pltpu.make_async_copy(sol, sol_hbm, out_sem.at[0]),
        pltpu.make_async_copy(res, res_hbm, out_sem.at[1]),
    )
    for store in stores:
        store.start()
    for store in stores:
        store.wait()


def times_link_by_three(link, half, adjoint):
    entry = {}
    sums = [half[n] + half[n + 1] for n in range(0, 12, 2)]
    out = []
    for spin in (0, 1):
        for row in range(3):
            one = two = three = None
            for col in range(3):
                key = (col, row) if adjoint else (row, col)
                if key not in entry:
                    entry[key] = link(3 * key[0] + key[1])
                u_re, u_plus, u_minus = entry[key]
                h_re, h_im = half[6 * spin + 2 * col], half[6 * spin + 2 * col + 1]
                if adjoint:
                    terms = u_re * sums[3 * spin + col], u_plus * h_re, u_minus * h_im
                else:
                    terms = u_re * sums[3 * spin + col], u_minus * h_re, u_plus * h_im
                if col == 0:
                    one, two, three = terms
                else:
                    one, two, three = one + terms[0], two + terms[1], three + terms[2]
            out += [one + three, one - two] if adjoint else [one - three, one + two]
    return out


def kernel(
    counts, src_hbm, links_hbm, sol, res,
    src, links, raw, inner, upd, rest, app, sent, got, in_sem, send_sem, recv_sem,
):
    ta, gx = lax.axis_index("ta"), lax.axis_index("gx")
    n_ta, n_gx = counts
    sides = (
        {"ta": lax.rem(ta + n_ta - 1, n_ta)}, {"ta": lax.rem(ta + 1, n_ta)},
        {"gx": lax.rem(gx + n_gx - 1, n_gx)}, {"gx": lax.rem(gx + 1, n_gx)},
    )

    barrier = pltpu.get_barrier_semaphore()
    for side in sides:
        pl.semaphore_signal(barrier, inc=1, device_id=side, device_id_type=MESH)
    loads = [pltpu.make_async_copy(src_hbm, src, in_sem.at[4])]
    for mu in range(4):
        part = pl.ds(18 * mu, 18)
        loads.append(pltpu.make_async_copy(links_hbm.at[part], links.at[part], in_sem.at[mu]))
    for load in loads:
        load.start()

    row = lax.broadcasted_iota(jnp.int32, (8, 128), 0)
    lane = lax.broadcasted_iota(jnp.int32, (8, 128), 1)
    x, y, z = row % 4, (lane // 16) % 4, lane % 16
    t = 2 * (lane // 64) + row // 4
    first = (lane // 64 + z // 4 + lax.rem(ta + gx, 2)) % 2 == 0
    low_lane, low_row = lane < 64, row < 4
    own = (first & low_lane, first & ~low_lane), (~first & low_lane, ~first & ~low_lane)
    coords = (t, x, y, z % 4)
    lane_row = lax.broadcasted_iota(jnp.int32, (128, 128), 0)
    lane_col = lax.broadcasted_iota(jnp.int32, (128, 128), 1)
    same_block = (lane_row % 16 // 4 == lane_col % 16 // 4).astype(jnp.bfloat16)
    inside = [jnp.where(coords[mu] == 3, 0.0, -0.5 / MASS_SHIFT) for mu in range(4)]
    face_up = [jnp.where(coords[mu] == 3, 0.5, 0.0) for mu in range(4)]
    face_down = [jnp.where(coords[mu] == 0, 0.5, 0.0) for mu in range(4)]

    def pack(ref, k, colour):
        a, b = ref[k, 0:8, :], ref[k, 8:16, :]
        there = lroll(jnp.where(low_lane, b, a), 64)
        own_a, own_b = own[colour]
        return jnp.where(own_a, a, jnp.where(own_b, b, there))

    def unpack(ref, k, p0, p1):
        here = jnp.where(first, p0, p1)
        there = lroll(jnp.where(first, p1, p0), 64)
        ref[k, 0:8, :] = jnp.where(low_lane, here, there)
        ref[k, 8:16, :] = jnp.where(low_lane, there, here)

    def pack_links(mu, colour):
        for k in range(9 * mu, 9 * mu + 9):
            re, im = pack(links, 2 * k, colour), pack(links, 2 * k + 1, colour)
            raw[colour, 2 * k], raw[colour, 2 * k + 1] = re, im
            re, im = re * inside[mu], im * inside[mu]
            inner[colour, 3 * k] = re
            inner[colour, 3 * k + 1] = im + re
            inner[colour, 3 * k + 2] = im - re

    def forward(v, mu):
        if mu == Z:
            return lroll(v, -1)
        if mu == Y:
            return lroll(v, -16)
        if mu == X:
            return sroll(v, -1)
        shifted = sroll(v, 4)
        return jnp.where(low_row, shifted, lroll(shifted, 64))

    def backward(v, mu):
        if mu == Z:
            return lroll(v, 1)
        if mu == Y:
            return lroll(v, 16)
        if mu == X:
            return sroll(v, 1)
        shifted = sroll(v, 4)
        return jnp.where(low_row, lroll(shifted, 64), shifted)

    def load(ref, colour):
        return [ref[colour, k] for k in range(24)]

    def store(ref, colour, values):
        for k in range(24):
            ref[colour, k] = values[k]

    def block_apply(v, colour):
        acc = v
        for mu in range(4):
            link = lambda e, mu=mu: [inner[colour, 27 * mu + 3 * e + n] for n in range(3)]
            half = [forward(h, mu) for h in project(v, mu, -1)]
            acc = reconstruct(acc, times_link_by_three(link, half, False), mu, -1)
            half = times_link_by_three(link, project(v, mu, 1), True)
            acc = reconstruct(acc, [backward(h, mu) for h in half], mu, 1)
        return acc

    def block_sums(stats):
        for shift in (4, 2, 1):
            stats = [v + sroll(v, shift) for v in stats]
        rows = jnp.where(row == 0, stats[0], jnp.where(row == 1, stats[1], stats[2]))
        pieces = []
        for _ in range(2):
            pieces.append(rows.astype(jnp.bfloat16).astype(jnp.float32))
            rows = rows - pieces[-1]
        split = jnp.concatenate(pieces).astype(jnp.bfloat16)
        sums = jnp.dot(split, same_block, preferred_element_type=jnp.float32)
        sums = sums[0:8] + sums[8:16]
        return [jnp.broadcast_to(sums[n : n + 1], (8, 128)) for n in range(3)]

    def coefficient(a, v):
        re = im = norm = None
        for k in range(0, 24, 2):
            a_re, a_im, v_re, v_im = a[k], a[k + 1], v[k], v[k + 1]
            terms = a_re * v_re + a_im * v_im, a_re * v_im - a_im * v_re, a_re * a_re + a_im * a_im
            if k == 0:
                re, im, norm = terms
            else:
                re, im, norm = re + terms[0], im + terms[1], norm + terms[2]
        re, im, norm = block_sums([re, im, norm])
        norm = norm + DENOM_EPSILON / MASS_SHIFT**2
        alpha = re / norm, im / norm
        return alpha, [value * (1 / MASS_SHIFT) for value in alpha]

    def plus_times(x, sign, alpha, y):
        out = []
        for k in range(0, 24, 2):
            re = alpha[0] * y[k] - alpha[1] * y[k + 1]
            im = alpha[0] * y[k + 1] + alpha[1] * y[k]
            if x is None:
                out += [re, im]
            elif sign > 0:
                out += [x[k] + re, x[k + 1] + im]
            else:
                out += [x[k] - re, x[k + 1] - im]
        return out

    def minimal_residual(colour):
        v = load(rest, colour)
        a = block_apply(v, colour)
        store(app, 0, a)
        b = block_apply(a, colour)
        alpha, scaled = coefficient(a, v)
        v, a = load(rest, colour), load(app, 0)
        update = plus_times(None, 1, scaled, v)
        v = plus_times(v, -1, alpha, a)
        a = plus_times(a, -1, alpha, b)
        store(app, 0, a)
        store(rest, colour, v)
        store(upd, colour, update)
        parts = {}
        for up in (False, True):
            halves = [t_half(w, colour, up) for w in (update, v)]
            turned = []
            for n in range(0, 12, 2):
                turned += [-halves[1][n + 1], halves[1][n]]
            parts[up] = [squeeze_t(half, up) for half in (*halves, turned)]
        alpha, scaled = coefficient(a, v)
        for up in (True, False):
            for m in range(3):
                so_far, along, across = (part[m] for part in parts[up])
                sent[colour, int(up), 8 * m : 8 * m + 8, :] = (
                    so_far + scaled[0] * along + scaled[1] * across
                )
        return alpha, scaled

    def finish(colour, scaled):
        update = plus_times(load(upd, colour), 1, scaled, load(rest, colour))
        store(upd, colour, update)
        return update

    def t_half(v, colour, up):
        half = project(v, T, 1 if up else -1)
        return times_link(lambda e: raw[colour, e], half, True) if up else half

    def squeeze_x(half, at):
        out = []
        for m in range(3):
            v = half[4 * m + at]
            for j in range(4):
                if j != at:
                    v = jnp.where(x == j, sroll(half[4 * m + j], j - at), v)
            out.append(v)
        return out

    def spread_x(three, to):
        return [sroll(three[k // 4], to - k % 4) for k in range(12)]

    def squeeze_t(half, high):
        rows = (row >= 4) if high else low_row
        lanes = (lane >= 64) if high else low_lane
        out = []
        for m in range(3):
            a, b, c, d = half[4 * m : 4 * m + 4]
            one = jnp.where(lanes, a, lroll(b, 64))
            two = jnp.where(lanes, c, lroll(d, 64))
            out.append(jnp.where(rows, one, sroll(two, 4)))
        return out

    def spread_t(three):
        out = []
        for v in three:
            s = sroll(v, 4)
            out += [lroll(s, 64), s, lroll(v, 64), v]
        return out

    def x_face(u, colour, slot):
        up = slot == 3
        half = project(u, X, 1 if up else -1)
        if up:
            half = times_link(lambda e: raw[colour, 18 + e], half, True)
        three = squeeze_x(half, 3 if up else 0)
        for m in range(3):
            sent[colour, slot, 8 * m : 8 * m + 8, :] = three[m]

    def send(colour, slots):
        @pl.when(ta >= 0)
        def _():
            for slot in slots:
                pltpu.make_async_remote_copy(
                    src_ref=sent.at[colour, slot],
                    dst_ref=got.at[colour, slot],
                    send_sem=send_sem.at[0],
                    recv_sem=recv_sem.at[colour, min(slot, 2)],
                    device_id=sides[slot],
                    device_id_type=MESH,
                ).start()

    def await_face(colour, slot, count=1):
        part = got.at[colour, pl.ds(slot, count)]
        pltpu.make_async_copy(part, part, recv_sem.at[colour, slot]).wait()

    def local_faces(u, colour, acc):
        other = 1 - colour
        for mu in (Y, Z):
            half = project(u, mu, -1)
            if mu == Y:
                half = [lroll(h, 48) for h in half]
            else:
                half = [jnp.where(z == 15, lroll(h, 15), lroll(h, -1)) for h in half]
            half = times_link(lambda e, mu=mu: raw[other, 18 * mu + e], half, False)
            acc = reconstruct(acc, [h * face_up[mu] for h in half], mu, -1)
            half = times_link(lambda e, mu=mu: raw[colour, 18 * mu + e], project(u, mu, 1), True)
            if mu == Y:
                half = [lroll(h, -48) for h in half]
            else:
                half = [jnp.where(z == 0, lroll(h, -15), lroll(h, 1)) for h in half]
            acc = reconstruct(acc, [h * face_down[mu] for h in half], mu, 1)
        return acc

    def add_face(acc, colour, slot):
        mu, up = slot // 2, slot % 2 == 1
        three = [got[colour, slot, 8 * m : 8 * m + 8, :] for m in range(3)]
        if up:
            half = spread_t(three) if mu == T else spread_x(three, 0)
            return reconstruct(acc, [h * face_down[mu] for h in half], mu, 1)
        half = spread_t(three) if mu == T else spread_x(three, 3)
        half = times_link(lambda e: raw[1 - colour, 18 * mu + e], half, False)
        return reconstruct(acc, [h * face_up[mu] for h in half], mu, -1)

    loads[0].wait()
    for k in range(24):
        rest[0, k] = pack(src, k, 0)
    for mu in range(4):
        loads[1 + mu].wait()
    for mu in range(4):
        pack_links(mu, 0)

    alpha, scaled = minimal_residual(0)
    pl.semaphore_wait(barrier, 4)
    send(0, (1, 0))
    update = finish(0, scaled)
    for slot in (3, 2):
        x_face(update, 0, slot)
    send(0, (3, 2))
    for k in range(24):
        rest[1, k] = pack(src, k, 1)
    for mu in range(4):
        pack_links(mu, 1)
    store(rest, 0, plus_times(load(rest, 0), -1, alpha, load(app, 0)))
    acc = local_faces(load(upd, 0), 0, load(rest, 1))
    store(rest, 1, acc)
    await_face(0, 2, 2)
    acc = add_face(add_face(load(rest, 1), 0, 2), 0, 3)
    store(rest, 1, acc)
    await_face(0, 1)
    await_face(0, 0)
    store(rest, 1, add_face(add_face(load(rest, 1), 0, 1), 0, 0))

    alpha, scaled = minimal_residual(1)
    send(1, (1, 0))
    update = finish(1, scaled)
    for slot in (3, 2):
        x_face(update, 1, slot)
        send(1, (slot,))
    store(rest, 1, plus_times(load(rest, 1), -1, alpha, load(app, 0)))
    for k in range(24):
        unpack(sol, k, upd[0, k], upd[1, k])
    store(rest, 0, local_faces(load(upd, 1), 1, load(rest, 0)))
    await_face(1, 2, 2)
    store(rest, 0, add_face(add_face(load(rest, 0), 1, 2), 1, 3))
    await_face(1, 0)
    acc = add_face(load(rest, 0), 1, 0)
    for k in range(24):
        unpack(res, k, acc[k], rest[1, k])
    pltpu.make_async_copy(sent, sent, send_sem.at[0]).wait()
    at_zero = jnp.where(first & low_row, 0.5, 0.0)
    await_face(1, 1)
    half = []
    for m in range(3):
        v = got[1, 1, 8 * m : 8 * m + 8, :]
        s = sroll(v, 4)
        v_far, s_far = lroll(v, 64), lroll(s, 64)
        half += [
            jnp.where(low_lane, s_far, s), jnp.where(low_lane, s, s_far),
            jnp.where(low_lane, v_far, v), jnp.where(low_lane, v, v_far),
        ]
    acc = [res[k, 0:8, :] for k in range(24)]
    acc = reconstruct(acc, [h * at_zero for h in half], T, 1)
    for k in range(24):
        res[k, 0:8, :] = acc[k]


def solution(mesh):
    counts = mesh.shape["ta"], mesh.shape["gx"]

    def local(source, gauge_links):
        spinor = pltpu.HBM((24, 16, 128), jnp.float32)
        vmem = lambda *shape: pltpu.VMEM(shape, jnp.float32)
        plain = pltpu.VMEM((24, 16, 128), jnp.float32)
        hbm, in_vmem = pl.BlockSpec(memory_space=pltpu.HBM), pl.BlockSpec(memory_space=pltpu.VMEM)
        out = pl.pallas_call(
            lambda *refs: kernel(counts, *refs),
            out_shape=(plain, plain),
            in_specs=[hbm, hbm],
            out_specs=(in_vmem, in_vmem),
            scratch_shapes=[
                vmem(24, 16, 128),
                vmem(72, 16, 128),
                vmem(2, 72, 8, 128),
                vmem(2, 108, 8, 128),
                vmem(2, 24, 8, 128),
                vmem(2, 24, 8, 128),
                vmem(1, 24, 8, 128),
                vmem(2, 4, 24, 128),
                vmem(2, 4, 24, 128),
                pltpu.SemaphoreType.DMA((5,)),
                pltpu.SemaphoreType.DMA((1,)),
                pltpu.SemaphoreType.DMA((2, 3)),
            ],
            compiler_params=pltpu.CompilerParams(
                collective_id=0, has_side_effects=True, vmem_limit_bytes=24 << 20
            ),
            name="schwarz",
        )(
            pltpu.with_memory_space_constraint(source.reshape(24, 16, 128), pltpu.HBM),
            pltpu.with_memory_space_constraint(gauge_links.reshape(72, 16, 128), pltpu.HBM),
        )
        out = pl.pallas_call(
            store_kernel,
            out_shape=(spinor, spinor),
            in_specs=[in_vmem, in_vmem],
            out_specs=(hbm, hbm),
            scratch_shapes=[pltpu.SemaphoreType.DMA((2,))],
            compiler_params=pltpu.CompilerParams(vmem_limit_bytes=4 << 20),
            name="store",
        )(*(pltpu.with_memory_space_constraint(value, pltpu.VMEM) for value in out))
        return tuple(value.reshape(24, 4, 4, 128) for value in out)

    return jax.shard_map(
        local,
        mesh=mesh,
        in_specs=(P(None, "ta", "gx", None), P(None, None, "ta", "gx", None)),
        out_specs=(P(None, "ta", "gx", None), P(None, "ta", "gx", None)),
        check_vma=False,
    )
```

```python
import jax
import jax.numpy as jnp
from jax import lax
from jax.experimental import pallas as pl
from jax.experimental.pallas import tpu as pltpu
from jax.sharding import PartitionSpec as P

MR_STEPS = 2
PERM = ((2, 3, 0, 1), (3, 2, 1, 0), (3, 2, 1, 0), (2, 3, 0, 1))
PHASE = (
    (1, 1, 1, 1),
    (1j, 1j, -1j, -1j),
    (-1, 1, 1, -1),
    (1j, -1j, -1j, 1j),
)
MASS_SHIFT = 4.1
DENOM_EPSILON = 1e-6
T, X, Y, Z = range(4)
MESH = pl.DeviceIdType.MESH


def lroll(v, shift):
    return pltpu.roll(v, shift % 128, 1)


def sroll(v, shift):
    shift %= 8
    return v if shift == 0 else pltpu.roll(v, shift, 0)


def plus_phase(x, phase, y):
    if phase == 1:
        return x[0] + y[0], x[1] + y[1]
    if phase == -1:
        return x[0] - y[0], x[1] - y[1]
    if phase == 1j:
        return x[0] - y[1], x[1] + y[0]
    return x[0] + y[1], x[1] - y[0]


def project(v, mu, parity):
    half = []
    for spin in (0, 1):
        phase, partner = parity * PHASE[mu][spin], PERM[mu][spin]
        for colour in range(3):
            at, other = 6 * spin + 2 * colour, 6 * partner + 2 * colour
            half += plus_phase((v[at], v[at + 1]), phase, (v[other], v[other + 1]))
    return half


def reconstruct(acc, half, mu, parity):
    acc = list(acc)
    for spin in range(4):
        phase, source = (1, spin) if spin < 2 else (parity * PHASE[mu][spin], PERM[mu][spin])
        for colour in range(3):
            at, other = 6 * spin + 2 * colour, 6 * source + 2 * colour
            acc[at], acc[at + 1] = plus_phase(
                (acc[at], acc[at + 1]), phase, (half[other], half[other + 1])
            )
    return acc


def times_link(link, half, adjoint):
    out = []
    entry = {}
    for spin in (0, 1):
        for row in range(3):
            re = im = None
            for col in range(3):
                key = 6 * col + 2 * row if adjoint else 6 * row + 2 * col
                if key not in entry:
                    entry[key] = link(key), link(key + 1)
                u_re, u_im = entry[key]
                h_re, h_im = half[6 * spin + 2 * col], half[6 * spin + 2 * col + 1]
                if adjoint:
                    re_term, im_term = u_re * h_re + u_im * h_im, u_re * h_im - u_im * h_re
                else:
                    re_term, im_term = u_re * h_re - u_im * h_im, u_re * h_im + u_im * h_re
                re = re_term if re is None else re + re_term
                im = im_term if im is None else im + im_term
            out += [re, im]
    return out


def store_kernel(sol, res, sol_hbm, res_hbm, out_sem):
    stores = (
        pltpu.make_async_copy(sol, sol_hbm, out_sem.at[0]),
        pltpu.make_async_copy(res, res_hbm, out_sem.at[1]),
    )
    for store in stores:
        store.start()
    for store in stores:
        store.wait()


def times_link_by_three(link, half, adjoint):
    entry = {}
    sums = [half[n] + half[n + 1] for n in range(0, 12, 2)]
    out = []
    for spin in (0, 1):
        for row in range(3):
            one = two = three = None
            for col in range(3):
                key = (col, row) if adjoint else (row, col)
                if key not in entry:
                    entry[key] = link(3 * key[0] + key[1])
                u_re, u_plus, u_minus = entry[key]
                h_re, h_im = half[6 * spin + 2 * col], half[6 * spin + 2 * col + 1]
                if adjoint:
                    terms = u_re * sums[3 * spin + col], u_plus * h_re, u_minus * h_im
                else:
                    terms = u_re * sums[3 * spin + col], u_minus * h_re, u_plus * h_im
                if col == 0:
                    one, two, three = terms
                else:
                    one, two, three = one + terms[0], two + terms[1], three + terms[2]
            out += [one + three, one - two] if adjoint else [one - three, one + two]
    return out


def kernel(
    counts, src_hbm, links_hbm, sol, res,
    src, links, raw, inner, upd, rest, app, sent, got, in_sem, send_sem, recv_sem,
):
    ta, gx = lax.axis_index("ta"), lax.axis_index("gx")
    n_ta, n_gx = counts
    sides = (
        {"ta": lax.rem(ta + n_ta - 1, n_ta)}, {"ta": lax.rem(ta + 1, n_ta)},
        {"gx": lax.rem(gx + n_gx - 1, n_gx)}, {"gx": lax.rem(gx + 1, n_gx)},
    )

    barrier = pltpu.get_barrier_semaphore()
    for side in sides:
        pl.semaphore_signal(barrier, inc=1, device_id=side, device_id_type=MESH)
    loads = [pltpu.make_async_copy(src_hbm, src, in_sem.at[4])]
    for mu in range(4):
        part = pl.ds(18 * mu, 18)
        loads.append(pltpu.make_async_copy(links_hbm.at[part], links.at[part], in_sem.at[mu]))
    for load in loads:
        load.start()

    row = lax.broadcasted_iota(jnp.int32, (8, 128), 0)
    lane = lax.broadcasted_iota(jnp.int32, (8, 128), 1)
    x, y, z = row % 4, (lane // 16) % 4, lane % 16
    t = 2 * (lane // 64) + row // 4
    first = (lane // 64 + z // 4 + lax.rem(ta + gx, 2)) % 2 == 0
    low_lane, low_row = lane < 64, row < 4
    lanes_of = (
        (first & low_lane, first & ~low_lane), (~first & low_lane, ~first & ~low_lane)
    )
    coords = (t, x, y, z % 4)
    lane_row = lax.broadcasted_iota(jnp.int32, (128, 128), 0)
    lane_col = lax.broadcasted_iota(jnp.int32, (128, 128), 1)
    same_block = (lane_row % 16 // 4 == lane_col % 16 // 4).astype(jnp.bfloat16)
    inside = [jnp.where(coords[mu] == 3, 0.0, -0.5 / MASS_SHIFT) for mu in range(4)]
    face_up = [jnp.where(coords[mu] == 3, 0.5, 0.0) for mu in range(4)]
    face_down = [jnp.where(coords[mu] == 0, 0.5, 0.0) for mu in range(4)]

    def pack(ref, k, colour):
        a, b = ref[k, 0:8, :], ref[k, 8:16, :]
        there = lroll(jnp.where(low_lane, b, a), 64)
        own_a, own_b = lanes_of[colour]
        return jnp.where(own_a, a, jnp.where(own_b, b, there))

    def unpack(ref, k, p0, p1):
        here = jnp.where(first, p0, p1)
        there = lroll(jnp.where(first, p1, p0), 64)
        ref[k, 0:8, :] = jnp.where(low_lane, here, there)
        ref[k, 8:16, :] = jnp.where(low_lane, there, here)

    def pack_links(mu, colour):
        for k in range(9 * mu, 9 * mu + 9):
            re, im = pack(links, 2 * k, colour), pack(links, 2 * k + 1, colour)
            raw[colour, 2 * k], raw[colour, 2 * k + 1] = re, im
            re, im = re * inside[mu], im * inside[mu]
            inner[colour, 3 * k] = re
            inner[colour, 3 * k + 1] = im + re
            inner[colour, 3 * k + 2] = im - re

    def forward(v, mu):
        if mu == Z:
            return lroll(v, -1)
        if mu == Y:
            return lroll(v, -16)
        if mu == X:
            return sroll(v, -1)
        shifted = sroll(v, 4)
        return jnp.where(low_row, shifted, lroll(shifted, 64))

    def backward(v, mu):
        if mu == Z:
            return lroll(v, 1)
        if mu == Y:
            return lroll(v, 16)
        if mu == X:
            return sroll(v, 1)
        shifted = sroll(v, 4)
        return jnp.where(low_row, lroll(shifted, 64), shifted)

    def load(ref, colour):
        return [ref[colour, k] for k in range(24)]

    def store(ref, colour, values):
        for k in range(24):
            ref[colour, k] = values[k]

    def block_apply(v, colour):
        acc = v
        for mu in range(4):
            link = lambda e, mu=mu: [inner[colour, 27 * mu + 3 * e + n] for n in range(3)]
            half = [forward(h, mu) for h in project(v, mu, -1)]
            acc = reconstruct(acc, times_link_by_three(link, half, False), mu, -1)
            half = times_link_by_three(link, project(v, mu, 1), True)
            acc = reconstruct(acc, [backward(h, mu) for h in half], mu, 1)
        return acc

    def block_sums(stats):
        for shift in (4, 2, 1):
            stats = [v + sroll(v, shift) for v in stats]
        rows = jnp.where(row == 0, stats[0], jnp.where(row == 1, stats[1], stats[2]))
        pieces = []
        for _ in range(2):
            pieces.append(rows.astype(jnp.bfloat16).astype(jnp.float32))
            rows = rows - pieces[-1]
        split = jnp.concatenate(pieces).astype(jnp.bfloat16)
        sums = jnp.dot(split, same_block, preferred_element_type=jnp.float32)
        sums = sums[0:8] + sums[8:16]
        return [jnp.broadcast_to(sums[n : n + 1], (8, 128)) for n in range(3)]

    def coefficient(a, v):
        re = im = norm = None
        for k in range(0, 24, 2):
            a_re, a_im, v_re, v_im = a[k], a[k + 1], v[k], v[k + 1]
            terms = a_re * v_re + a_im * v_im, a_re * v_im - a_im * v_re, a_re * a_re + a_im * a_im
            if k == 0:
                re, im, norm = terms
            else:
                re, im, norm = re + terms[0], im + terms[1], norm + terms[2]
        re, im, norm = block_sums([re, im, norm])
        norm = norm + DENOM_EPSILON / MASS_SHIFT**2
        alpha = re / norm, im / norm
        return alpha, [value * (1 / MASS_SHIFT) for value in alpha]

    def plus_times(x, sign, alpha, y):
        out = []
        for k in range(0, 24, 2):
            re = alpha[0] * y[k] - alpha[1] * y[k + 1]
            im = alpha[0] * y[k + 1] + alpha[1] * y[k]
            if x is None:
                out += [re, im]
            elif sign > 0:
                out += [x[k] + re, x[k + 1] + im]
            else:
                out += [x[k] - re, x[k + 1] - im]
        return out

    def minimal_residual(colour):
        v = load(rest, colour)
        a = block_apply(v, colour)
        store(app, 0, a)
        b = block_apply(a, colour)
        alpha, scaled = coefficient(a, v)
        v, a = load(rest, colour), load(app, 0)
        update = plus_times(None, 1, scaled, v)
        v = plus_times(v, -1, alpha, a)
        a = plus_times(a, -1, alpha, b)
        store(app, 0, a)
        store(rest, colour, v)
        store(upd, colour, update)
        parts = {}
        for up in (False, True):
            halves = [t_half(w, colour, up) for w in (update, v)]
            turned = []
            for n in range(0, 12, 2):
                turned += [-halves[1][n + 1], halves[1][n]]
            parts[up] = [squeeze_t(half, up) for half in (*halves, turned)]
        alpha, scaled = coefficient(a, v)
        for up in (True, False):
            for m in range(3):
                so_far, along, across = (part[m] for part in parts[up])
                sent[colour, int(up), 8 * m : 8 * m + 8, :] = (
                    so_far + scaled[0] * along + scaled[1] * across
                )
        return alpha, scaled

    def finish(colour, scaled):
        update = plus_times(load(upd, colour), 1, scaled, load(rest, colour))
        store(upd, colour, update)
        return update

    def t_half(v, colour, up):
        half = project(v, T, 1 if up else -1)
        return times_link(lambda e: raw[colour, e], half, True) if up else half

    def squeeze_x(half, at):
        out = []
        for m in range(3):
            v = half[4 * m + at]
            for j in range(4):
                if j != at:
                    v = jnp.where(x == j, sroll(half[4 * m + j], j - at), v)
            out.append(v)
        return out

    def spread_x(three, to):
        return [sroll(three[k // 4], to - k % 4) for k in range(12)]

    def squeeze_t(half, high):
        rows = (row >= 4) if high else low_row
        lanes = (lane >= 64) if high else low_lane
        out = []
        for m in range(3):
            a, b, c, d = half[4 * m : 4 * m + 4]
            one = jnp.where(lanes, a, lroll(b, 64))
            two = jnp.where(lanes, c, lroll(d, 64))
            out.append(jnp.where(rows, one, sroll(two, 4)))
        return out

    def spread_t(three):
        out = []
        for v in three:
            s = sroll(v, 4)
            out += [lroll(s, 64), s, lroll(v, 64), v]
        return out

    def x_face(u, colour, slot):
        up = slot == 3
        half = project(u, X, 1 if up else -1)
        if up:
            half = times_link(lambda e: raw[colour, 18 + e], half, True)
        three = squeeze_x(half, 3 if up else 0)
        for m in range(3):
            sent[colour, slot, 8 * m : 8 * m + 8, :] = three[m]

    def send(colour, slots):
        @pl.when(ta >= 0)
        def _():
            for slot in slots:
                pltpu.make_async_remote_copy(
                    src_ref=sent.at[colour, slot],
                    dst_ref=got.at[colour, slot],
                    send_sem=send_sem.at[0],
                    recv_sem=recv_sem.at[colour, slot],
                    device_id=sides[slot],
                    device_id_type=MESH,
                ).start()

    def await_face(colour, slot):
        part = got.at[colour, slot]
        pltpu.make_async_copy(part, part, recv_sem.at[colour, slot]).wait()

    def local_faces(u, colour, acc):
        other = 1 - colour
        for mu in (Y, Z):
            half = project(u, mu, -1)
            if mu == Y:
                half = [lroll(h, 48) for h in half]
            else:
                half = [jnp.where(z == 15, lroll(h, 15), lroll(h, -1)) for h in half]
            half = times_link(lambda e, mu=mu: raw[other, 18 * mu + e], half, False)
            acc = reconstruct(acc, [h * face_up[mu] for h in half], mu, -1)
            half = times_link(lambda e, mu=mu: raw[colour, 18 * mu + e], project(u, mu, 1), True)
            if mu == Y:
                half = [lroll(h, -48) for h in half]
            else:
                half = [jnp.where(z == 0, lroll(h, -15), lroll(h, 1)) for h in half]
            acc = reconstruct(acc, [h * face_down[mu] for h in half], mu, 1)
        return acc

    def add_face(acc, colour, slot):
        mu, up = slot // 2, slot % 2 == 1
        three = [got[colour, slot, 8 * m : 8 * m + 8, :] for m in range(3)]
        if up:
            half = spread_t(three) if mu == T else spread_x(three, 0)
            return reconstruct(acc, [h * face_down[mu] for h in half], mu, 1)
        half = spread_t(three) if mu == T else spread_x(three, 3)
        half = times_link(lambda e: raw[1 - colour, 18 * mu + e], half, False)
        return reconstruct(acc, [h * face_up[mu] for h in half], mu, -1)

    loads[0].wait()
    for k in range(24):
        rest[0, k] = pack(src, k, 0)
    for mu in range(4):
        loads[1 + mu].wait()
    for mu in range(4):
        pack_links(mu, 0)

    alpha, scaled = minimal_residual(0)
    pl.semaphore_wait(barrier, 4)
    send(0, (1, 0))
    update = finish(0, scaled)
    for slot in (3, 2):
        x_face(update, 0, slot)
    send(0, (3, 2))
    for k in range(24):
        rest[1, k] = pack(src, k, 1)
    for mu in range(4):
        pack_links(mu, 1)
    store(rest, 0, plus_times(load(rest, 0), -1, alpha, load(app, 0)))
    acc = local_faces(load(upd, 0), 0, load(rest, 1))
    store(rest, 1, acc)
    await_face(0, 2)
    await_face(0, 3)
    acc = add_face(add_face(load(rest, 1), 0, 2), 0, 3)
    store(rest, 1, acc)
    await_face(0, 1)
    await_face(0, 0)
    store(rest, 1, add_face(add_face(load(rest, 1), 0, 1), 0, 0))

    alpha, scaled = minimal_residual(1)
    send(1, (1, 0))
    update = finish(1, scaled)
    for slot in (3, 2):
        x_face(update, 1, slot)
        send(1, (slot,))
    store(rest, 1, plus_times(load(rest, 1), -1, alpha, load(app, 0)))
    for k in range(24):
        unpack(sol, k, upd[0, k], upd[1, k])
    store(rest, 0, local_faces(load(upd, 1), 1, load(rest, 0)))
    await_face(1, 0)
    store(rest, 0, add_face(load(rest, 0), 1, 0))
    await_face(1, 2)
    acc = add_face(load(rest, 0), 1, 2)
    for k in range(24):
        unpack(res, k, acc[k], rest[1, k])
    pltpu.make_async_copy(sent, sent, send_sem.at[0]).wait()
    at_zero = jnp.where(first & low_row, 0.5, 0.0)
    await_face(1, 1)
    half = []
    for m in range(3):
        v = got[1, 1, 8 * m : 8 * m + 8, :]
        s = sroll(v, 4)
        v_far, s_far = lroll(v, 64), lroll(s, 64)
        half += [
            jnp.where(low_lane, s_far, s), jnp.where(low_lane, s, s_far),
            jnp.where(low_lane, v_far, v), jnp.where(low_lane, v, v_far),
        ]
    acc = [res[k, 0:8, :] for k in range(24)]
    acc = reconstruct(acc, [h * at_zero for h in half], T, 1)
    for k in range(24):
        res[k, 0:8, :] = acc[k]
    at_zero = jnp.where(first & (x == 0), 0.5, 0.0)
    await_face(1, 3)
    near = spread_x([got[1, 3, 8 * m : 8 * m + 8, :] for m in range(3)], 0)
    far = [lroll(h, 64) for h in near]
    for rows, own, other in ((slice(0, 8), near, far), (slice(8, 16), far, near)):
        half = [jnp.where(low_lane, p, q) * at_zero for p, q in zip(own, other)]
        acc = reconstruct([res[k, rows, :] for k in range(24)], half, X, 1)
        for k in range(24):
            res[k, rows, :] = acc[k]


def solution(mesh):
    counts = mesh.shape["ta"], mesh.shape["gx"]

    def local(source, gauge_links):
        spinor = pltpu.HBM((24, 16, 128), jnp.float32)
        vmem = lambda *shape: pltpu.VMEM(shape, jnp.float32)
        plain = pltpu.VMEM((24, 16, 128), jnp.float32)
        hbm, in_vmem = pl.BlockSpec(memory_space=pltpu.HBM), pl.BlockSpec(memory_space=pltpu.VMEM)
        out = pl.pallas_call(
            lambda *refs: kernel(counts, *refs),
            out_shape=(plain, plain),
            in_specs=[hbm, hbm],
            out_specs=(in_vmem, in_vmem),
            scratch_shapes=[
                vmem(24, 16, 128),
                vmem(72, 16, 128),
                vmem(2, 72, 8, 128),
                vmem(2, 108, 8, 128),
                vmem(2, 24, 8, 128),
                vmem(2, 24, 8, 128),
                vmem(1, 24, 8, 128),
                vmem(2, 4, 24, 128),
                vmem(2, 4, 24, 128),
                pltpu.SemaphoreType.DMA((5,)),
                pltpu.SemaphoreType.DMA((1,)),
                pltpu.SemaphoreType.DMA((2, 4)),
            ],
            compiler_params=pltpu.CompilerParams(
                collective_id=0, has_side_effects=True, vmem_limit_bytes=24 << 20
            ),
            name="schwarz",
        )(
            pltpu.with_memory_space_constraint(source.reshape(24, 16, 128), pltpu.HBM),
            pltpu.with_memory_space_constraint(gauge_links.reshape(72, 16, 128), pltpu.HBM),
        )
        out = pl.pallas_call(
            store_kernel,
            out_shape=(spinor, spinor),
            in_specs=[in_vmem, in_vmem],
            out_specs=(hbm, hbm),
            scratch_shapes=[pltpu.SemaphoreType.DMA((2,))],
            compiler_params=pltpu.CompilerParams(vmem_limit_bytes=4 << 20),
            name="store",
        )(*(pltpu.with_memory_space_constraint(value, pltpu.VMEM) for value in out))
        return tuple(value.reshape(24, 4, 4, 128) for value in out)

    return jax.shard_map(
        local,
        mesh=mesh,
        in_specs=(P(None, "ta", "gx", None), P(None, None, "ta", "gx", None)),
        out_specs=(P(None, "ta", "gx", None), P(None, "ta", "gx", None)),
        check_vma=False,
    )
```

```python
import jax
import jax.numpy as jnp
from jax import lax
from jax.experimental import pallas as pl
from jax.experimental.pallas import tpu as pltpu
from jax.sharding import PartitionSpec as P

MR_STEPS = 2
PERM = ((2, 3, 0, 1), (3, 2, 1, 0), (3, 2, 1, 0), (2, 3, 0, 1))
PHASE = (
    (1, 1, 1, 1),
    (1j, 1j, -1j, -1j),
    (-1, 1, 1, -1),
    (1j, -1j, -1j, 1j),
)
MASS_SHIFT = 4.1
DENOM_EPSILON = 1e-6
T, X, Y, Z = range(4)
MESH = pl.DeviceIdType.MESH


def lroll(v, shift):
    return pltpu.roll(v, shift % 128, 1)


def sroll(v, shift):
    shift %= 8
    return v if shift == 0 else pltpu.roll(v, shift, 0)


def plus_phase(x, phase, y):
    if phase == 1:
        return x[0] + y[0], x[1] + y[1]
    if phase == -1:
        return x[0] - y[0], x[1] - y[1]
    if phase == 1j:
        return x[0] - y[1], x[1] + y[0]
    return x[0] + y[1], x[1] - y[0]


def project(v, mu, parity):
    half = []
    for spin in (0, 1):
        phase, partner = parity * PHASE[mu][spin], PERM[mu][spin]
        for colour in range(3):
            at, other = 6 * spin + 2 * colour, 6 * partner + 2 * colour
            half += plus_phase((v[at], v[at + 1]), phase, (v[other], v[other + 1]))
    return half


def reconstruct(acc, half, mu, parity):
    acc = list(acc)
    for spin in range(4):
        phase, source = (1, spin) if spin < 2 else (parity * PHASE[mu][spin], PERM[mu][spin])
        for colour in range(3):
            at, other = 6 * spin + 2 * colour, 6 * source + 2 * colour
            acc[at], acc[at + 1] = plus_phase(
                (acc[at], acc[at + 1]), phase, (half[other], half[other + 1])
            )
    return acc


def times_link(link, half, adjoint):
    out = []
    entry = {}
    for spin in (0, 1):
        for row in range(3):
            re = im = None
            for col in range(3):
                key = 6 * col + 2 * row if adjoint else 6 * row + 2 * col
                if key not in entry:
                    entry[key] = link(key), link(key + 1)
                u_re, u_im = entry[key]
                h_re, h_im = half[6 * spin + 2 * col], half[6 * spin + 2 * col + 1]
                if adjoint:
                    re_term, im_term = u_re * h_re + u_im * h_im, u_re * h_im - u_im * h_re
                else:
                    re_term, im_term = u_re * h_re - u_im * h_im, u_re * h_im + u_im * h_re
                re = re_term if re is None else re + re_term
                im = im_term if im is None else im + im_term
            out += [re, im]
    return out


def store_kernel(sol, res, sol_hbm, res_hbm, out_sem):
    stores = (
        pltpu.make_async_copy(sol, sol_hbm, out_sem.at[0]),
        pltpu.make_async_copy(res, res_hbm, out_sem.at[1]),
    )
    for store in stores:
        store.start()
    for store in stores:
        store.wait()


def times_link_by_three(link, half, adjoint):
    entry = {}
    sums = [half[n] + half[n + 1] for n in range(0, 12, 2)]
    out = []
    for spin in (0, 1):
        for row in range(3):
            one = two = three = None
            for col in range(3):
                key = (col, row) if adjoint else (row, col)
                if key not in entry:
                    entry[key] = link(3 * key[0] + key[1])
                u_re, u_plus, u_minus = entry[key]
                h_re, h_im = half[6 * spin + 2 * col], half[6 * spin + 2 * col + 1]
                if adjoint:
                    terms = u_re * sums[3 * spin + col], u_plus * h_re, u_minus * h_im
                else:
                    terms = u_re * sums[3 * spin + col], u_minus * h_re, u_plus * h_im
                if col == 0:
                    one, two, three = terms
                else:
                    one, two, three = one + terms[0], two + terms[1], three + terms[2]
            out += [one + three, one - two] if adjoint else [one - three, one + two]
    return out


def kernel(
    counts, src_hbm, links_hbm, sol, res,
    src, links, raw, inner, upd, rest, app, sent, got, in_sem, send_sem, recv_sem,
):
    ta, gx = lax.axis_index("ta"), lax.axis_index("gx")
    n_ta, n_gx = counts
    sides = (
        {"ta": lax.rem(ta + n_ta - 1, n_ta)}, {"ta": lax.rem(ta + 1, n_ta)},
        {"gx": lax.rem(gx + n_gx - 1, n_gx)}, {"gx": lax.rem(gx + 1, n_gx)},
    )

    barrier = pltpu.get_barrier_semaphore()
    for side in sides:
        pl.semaphore_signal(barrier, inc=1, device_id=side, device_id_type=MESH)
    loads = [pltpu.make_async_copy(src_hbm, src, in_sem.at[4])]
    for mu in range(4):
        part = pl.ds(18 * mu, 18)
        loads.append(pltpu.make_async_copy(links_hbm.at[part], links.at[part], in_sem.at[mu]))
    for load in loads:
        load.start()

    row = lax.broadcasted_iota(jnp.int32, (8, 128), 0)
    lane = lax.broadcasted_iota(jnp.int32, (8, 128), 1)
    x, y, z = row % 4, (lane // 16) % 4, lane % 16
    t = 2 * (lane // 64) + row // 4
    first = (lane // 64 + z // 4 + lax.rem(ta + gx, 2)) % 2 == 0
    low_lane, low_row = lane < 64, row < 4
    lanes_of = (
        (first & low_lane, first & ~low_lane), (~first & low_lane, ~first & ~low_lane)
    )
    coords = (t, x, y, z % 4)
    lane_row = lax.broadcasted_iota(jnp.int32, (128, 128), 0)
    lane_col = lax.broadcasted_iota(jnp.int32, (128, 128), 1)
    same_block = (lane_row % 16 // 4 == lane_col % 16 // 4).astype(jnp.bfloat16)
    inside = [jnp.where(coords[mu] == 3, 0.0, -0.5 / MASS_SHIFT) for mu in range(4)]
    face_up = [jnp.where(coords[mu] == 3, 0.5, 0.0) for mu in range(4)]
    face_down = [jnp.where(coords[mu] == 0, 0.5, 0.0) for mu in range(4)]

    def pack(ref, k, colour):
        a, b = ref[k, 0:8, :], ref[k, 8:16, :]
        there = lroll(jnp.where(low_lane, b, a), 64)
        own_a, own_b = lanes_of[colour]
        return jnp.where(own_a, a, jnp.where(own_b, b, there))

    def unpack(ref, k, p0, p1):
        here = jnp.where(first, p0, p1)
        there = lroll(jnp.where(first, p1, p0), 64)
        ref[k, 0:8, :] = jnp.where(low_lane, here, there)
        ref[k, 8:16, :] = jnp.where(low_lane, there, here)

    def pack_links(mu, colour):
        for k in range(9 * mu, 9 * mu + 9):
            re, im = pack(links, 2 * k, colour), pack(links, 2 * k + 1, colour)
            raw[colour, 2 * k], raw[colour, 2 * k + 1] = re, im
            re, im = re * inside[mu], im * inside[mu]
            inner[colour, 3 * k] = re
            inner[colour, 3 * k + 1] = im + re
            inner[colour, 3 * k + 2] = im - re

    def forward(v, mu):
        if mu == Z:
            return lroll(v, -1)
        if mu == Y:
            return lroll(v, -16)
        if mu == X:
            return sroll(v, -1)
        shifted = sroll(v, 4)
        return jnp.where(low_row, shifted, lroll(shifted, 64))

    def backward(v, mu):
        if mu == Z:
            return lroll(v, 1)
        if mu == Y:
            return lroll(v, 16)
        if mu == X:
            return sroll(v, 1)
        shifted = sroll(v, 4)
        return jnp.where(low_row, lroll(shifted, 64), shifted)

    def load(ref, colour):
        return [ref[colour, k] for k in range(24)]

    def store(ref, colour, values):
        for k in range(24):
            ref[colour, k] = values[k]

    def block_apply(v, colour):
        acc = v
        for mu in range(4):
            link = lambda e, mu=mu: [inner[colour, 27 * mu + 3 * e + n] for n in range(3)]
            half = [forward(h, mu) for h in project(v, mu, -1)]
            acc = reconstruct(acc, times_link_by_three(link, half, False), mu, -1)
            half = times_link_by_three(link, project(v, mu, 1), True)
            acc = reconstruct(acc, [backward(h, mu) for h in half], mu, 1)
        return acc

    def block_sums(stats):
        rows = jnp.concatenate(stats)
        high = rows.astype(jnp.bfloat16)
        low = (rows - high.astype(jnp.float32)).astype(jnp.bfloat16)
        split = jnp.concatenate([high.astype(jnp.float32), low.astype(jnp.float32)]).astype(jnp.bfloat16)
        sums = jnp.dot(split, same_block, preferred_element_type=jnp.float32)
        stats = [sums[8 * n : 8 * n + 8] + sums[24 + 8 * n : 32 + 8 * n] for n in range(3)]
        for shift in (4, 2, 1):
            stats = [v + sroll(v, shift) for v in stats]
        return stats

    def coefficient(a, v):
        re = im = norm = None
        for k in range(0, 24, 2):
            a_re, a_im, v_re, v_im = a[k], a[k + 1], v[k], v[k + 1]
            terms = a_re * v_re + a_im * v_im, a_re * v_im - a_im * v_re, a_re * a_re + a_im * a_im
            if k == 0:
                re, im, norm = terms
            else:
                re, im, norm = re + terms[0], im + terms[1], norm + terms[2]
        re, im, norm = block_sums([re, im, norm])
        norm = norm + DENOM_EPSILON / MASS_SHIFT**2
        alpha = re / norm, im / norm
        return alpha, [value * (1 / MASS_SHIFT) for value in alpha]

    def plus_times(x, sign, alpha, y):
        out = []
        for k in range(0, 24, 2):
            re = alpha[0] * y[k] - alpha[1] * y[k + 1]
            im = alpha[0] * y[k + 1] + alpha[1] * y[k]
            if x is None:
                out += [re, im]
            elif sign > 0:
                out += [x[k] + re, x[k + 1] + im]
            else:
                out += [x[k] - re, x[k + 1] - im]
        return out

    def minimal_residual(colour):
        v = load(rest, colour)
        a = block_apply(v, colour)
        store(app, 0, a)
        b = block_apply(a, colour)
        alpha, scaled = coefficient(a, v)
        v, a = load(rest, colour), load(app, 0)
        update = plus_times(None, 1, scaled, v)
        v = plus_times(v, -1, alpha, a)
        a = plus_times(a, -1, alpha, b)
        store(app, 0, a)
        store(rest, colour, v)
        store(upd, colour, update)
        parts = {}
        for up in (False, True):
            halves = [t_half(w, colour, up) for w in (update, v)]
            turned = []
            for n in range(0, 12, 2):
                turned += [-halves[1][n + 1], halves[1][n]]
            parts[up] = [squeeze_t(half, up) for half in (*halves, turned)]
        alpha, scaled = coefficient(a, v)
        for up in (True, False):
            for m in range(3):
                so_far, along, across = (part[m] for part in parts[up])
                sent[colour, int(up), 8 * m : 8 * m + 8, :] = (
                    so_far + scaled[0] * along + scaled[1] * across
                )
        return alpha, scaled

    def finish(colour, scaled):
        update = plus_times(load(upd, colour), 1, scaled, load(rest, colour))
        store(upd, colour, update)
        return update

    def t_half(v, colour, up):
        half = project(v, T, 1 if up else -1)
        return times_link(lambda e: raw[colour, e], half, True) if up else half

    def squeeze_x(half, at):
        out = []
        for m in range(3):
            v = half[4 * m + at]
            for j in range(4):
                if j != at:
                    v = jnp.where(x == j, sroll(half[4 * m + j], j - at), v)
            out.append(v)
        return out

    def spread_x(three, to):
        return [sroll(three[k // 4], to - k % 4) for k in range(12)]

    def squeeze_t(half, high):
        rows = (row >= 4) if high else low_row
        lanes = (lane >= 64) if high else low_lane
        out = []
        for m in range(3):
            a, b, c, d = half[4 * m : 4 * m + 4]
            one = jnp.where(lanes, a, lroll(b, 64))
            two = jnp.where(lanes, c, lroll(d, 64))
            out.append(jnp.where(rows, one, sroll(two, 4)))
        return out

    def spread_t(three):
        out = []
        for v in three:
            s = sroll(v, 4)
            out += [lroll(s, 64), s, lroll(v, 64), v]
        return out

    def x_face(u, colour, slot):
        up = slot == 3
        half = project(u, X, 1 if up else -1)
        if up:
            half = times_link(lambda e: raw[colour, 18 + e], half, True)
        three = squeeze_x(half, 3 if up else 0)
        for m in range(3):
            sent[colour, slot, 8 * m : 8 * m + 8, :] = three[m]

    def send(colour, slots):
        @pl.when(ta >= 0)
        def _():
            for slot in slots:
                pltpu.make_async_remote_copy(
                    src_ref=sent.at[colour, slot],
                    dst_ref=got.at[colour, slot],
                    send_sem=send_sem.at[0],
                    recv_sem=recv_sem.at[colour, slot],
                    device_id=sides[slot],
                    device_id_type=MESH,
                ).start()

    def await_face(colour, slot):
        part = got.at[colour, slot]
        pltpu.make_async_copy(part, part, recv_sem.at[colour, slot]).wait()

    def local_faces(u, colour, acc):
        other = 1 - colour
        for mu in (Y, Z):
            half = project(u, mu, -1)
            if mu == Y:
                half = [lroll(h, 48) for h in half]
            else:
                half = [jnp.where(z == 15, lroll(h, 15), lroll(h, -1)) for h in half]
            half = times_link(lambda e, mu=mu: raw[other, 18 * mu + e], half, False)
            acc = reconstruct(acc, [h * face_up[mu] for h in half], mu, -1)
            half = times_link(lambda e, mu=mu: raw[colour, 18 * mu + e], project(u, mu, 1), True)
            if mu == Y:
                half = [lroll(h, -48) for h in half]
            else:
                half = [jnp.where(z == 0, lroll(h, -15), lroll(h, 1)) for h in half]
            acc = reconstruct(acc, [h * face_down[mu] for h in half], mu, 1)
        return acc

    def add_face(acc, colour, slot):
        mu, up = slot // 2, slot % 2 == 1
        three = [got[colour, slot, 8 * m : 8 * m + 8, :] for m in range(3)]
        if up:
            half = spread_t(three) if mu == T else spread_x(three, 0)
            return reconstruct(acc, [h * face_down[mu] for h in half], mu, 1)
        half = spread_t(three) if mu == T else spread_x(three, 3)
        half = times_link(lambda e: raw[1 - colour, 18 * mu + e], half, False)
        return reconstruct(acc, [h * face_up[mu] for h in half], mu, -1)

    loads[0].wait()
    for k in range(24):
        rest[0, k] = pack(src, k, 0)
    for mu in range(4):
        loads[1 + mu].wait()
    for mu in range(4):
        pack_links(mu, 0)

    alpha, scaled = minimal_residual(0)
    pl.semaphore_wait(barrier, 4)
    send(0, (1, 0))
    update = finish(0, scaled)
    for slot in (3, 2):
        x_face(update, 0, slot)
    send(0, (3, 2))
    for k in range(24):
        rest[1, k] = pack(src, k, 1)
    for mu in range(4):
        pack_links(mu, 1)
    store(rest, 0, plus_times(load(rest, 0), -1, alpha, load(app, 0)))
    acc = local_faces(load(upd, 0), 0, load(rest, 1))
    store(rest, 1, acc)
    await_face(0, 2)
    await_face(0, 3)
    acc = add_face(add_face(load(rest, 1), 0, 2), 0, 3)
    store(rest, 1, acc)
    await_face(0, 1)
    await_face(0, 0)
    store(rest, 1, add_face(add_face(load(rest, 1), 0, 1), 0, 0))

    alpha, scaled = minimal_residual(1)
    send(1, (1, 0))
    update = finish(1, scaled)
    for slot in (3, 2):
        x_face(update, 1, slot)
        send(1, (slot,))
    store(rest, 1, plus_times(load(rest, 1), -1, alpha, load(app, 0)))
    for k in range(24):
        unpack(sol, k, upd[0, k], upd[1, k])
    store(rest, 0, local_faces(load(upd, 1), 1, load(rest, 0)))
    await_face(1, 0)
    store(rest, 0, add_face(load(rest, 0), 1, 0))
    await_face(1, 2)
    acc = add_face(load(rest, 0), 1, 2)
    for k in range(24):
        unpack(res, k, acc[k], rest[1, k])
    pltpu.make_async_copy(sent, sent, send_sem.at[0]).wait()
    at_zero = jnp.where(first & low_row, 0.5, 0.0)
    await_face(1, 1)
    half = []
    for m in range(3):
        v = got[1, 1, 8 * m : 8 * m + 8, :]
        s = sroll(v, 4)
        v_far, s_far = lroll(v, 64), lroll(s, 64)
        half += [
            jnp.where(low_lane, s_far, s), jnp.where(low_lane, s, s_far),
            jnp.where(low_lane, v_far, v), jnp.where(low_lane, v, v_far),
        ]
    acc = [res[k, 0:8, :] for k in range(24)]
    acc = reconstruct(acc, [h * at_zero for h in half], T, 1)
    for k in range(24):
        res[k, 0:8, :] = acc[k]
    at_zero = jnp.where(first & (x == 0), 0.5, 0.0)
    await_face(1, 3)
    near = spread_x([got[1, 3, 8 * m : 8 * m + 8, :] for m in range(3)], 0)
    far = [lroll(h, 64) for h in near]
    for rows, own, other in ((slice(0, 8), near, far), (slice(8, 16), far, near)):
        half = [jnp.where(low_lane, p, q) * at_zero for p, q in zip(own, other)]
        acc = reconstruct([res[k, rows, :] for k in range(24)], half, X, 1)
        for k in range(24):
            res[k, rows, :] = acc[k]


def solution(mesh):
    counts = mesh.shape["ta"], mesh.shape["gx"]

    def local(source, gauge_links):
        spinor = pltpu.HBM((24, 16, 128), jnp.float32)
        vmem = lambda *shape: pltpu.VMEM(shape, jnp.float32)
        plain = pltpu.VMEM((24, 16, 128), jnp.float32)
        hbm, in_vmem = pl.BlockSpec(memory_space=pltpu.HBM), pl.BlockSpec(memory_space=pltpu.VMEM)
        out = pl.pallas_call(
            lambda *refs: kernel(counts, *refs),
            out_shape=(plain, plain),
            in_specs=[hbm, hbm],
            out_specs=(in_vmem, in_vmem),
            scratch_shapes=[
                vmem(24, 16, 128),
                vmem(72, 16, 128),
                vmem(2, 72, 8, 128),
                vmem(2, 108, 8, 128),
                vmem(2, 24, 8, 128),
                vmem(2, 24, 8, 128),
                vmem(1, 24, 8, 128),
                vmem(2, 4, 24, 128),
                vmem(2, 4, 24, 128),
                pltpu.SemaphoreType.DMA((5,)),
                pltpu.SemaphoreType.DMA((1,)),
                pltpu.SemaphoreType.DMA((2, 4)),
            ],
            compiler_params=pltpu.CompilerParams(
                collective_id=0, has_side_effects=True, vmem_limit_bytes=24 << 20
            ),
            name="schwarz",
        )(
            pltpu.with_memory_space_constraint(source.reshape(24, 16, 128), pltpu.HBM),
            pltpu.with_memory_space_constraint(gauge_links.reshape(72, 16, 128), pltpu.HBM),
        )
        out = pl.pallas_call(
            store_kernel,
            out_shape=(spinor, spinor),
            in_specs=[in_vmem, in_vmem],
            out_specs=(hbm, hbm),
            scratch_shapes=[pltpu.SemaphoreType.DMA((2,))],
            compiler_params=pltpu.CompilerParams(vmem_limit_bytes=4 << 20),
            name="store",
        )(*(pltpu.with_memory_space_constraint(value, pltpu.VMEM) for value in out))
        return tuple(value.reshape(24, 4, 4, 128) for value in out)

    return jax.shard_map(
        local,
        mesh=mesh,
        in_specs=(P(None, "ta", "gx", None), P(None, None, "ta", "gx", None)),
        out_specs=(P(None, "ta", "gx", None), P(None, "ta", "gx", None)),
        check_vma=False,
    )
```
